32 devices in a mesh: req: 4 (over z), exp: 8 (over y, x, core).
Axes of the slice: x: 2, y: 2, z: 4, core: 2. Of those that a mesh axis runs over, the one named last changes fastest.
Arguments:
- queries: bfloat16 [32, 64, 2048], P(('req', 'exp'))
- new_kv: bfloat16 [32, 64, 2, 2048], P(('req', 'exp')), may hold values from -6 to 6
- cache: bfloat16 [32, 512, 2, 2048], P(('req', 'exp'))
- lengths: int32 [32], P(('req', 'exp')), may hold values from 8 to 448
- residual: bfloat16 [32, 64, 2048], P(('req', 'exp')), may hold values from -6 to 6
- out_weight: bfloat16 [2048, 2048], replicated, may hold values from -0.125 to 0.125
- norm_gain: float32 [2048], replicated, may hold values from 0.1 to 1.9
- expert_ids: int32 [32, 64, 8], P(('req', 'exp')), may hold values from 0 to 15, all different within a row; in each aligned block of 64 rows (0 to 63, 64 to 127, ..., all dimensions but the last counted through in order) at most 40 rows name the same one
- gates: float32 [32, 64, 8], P(('req', 'exp')), may hold values from 0.1 to 1
- w_gate: bfloat16 [32, 2048, 512], P(('req', 'exp')), may hold values from -0.125 to 0.125
- w_up: bfloat16 [32, 2048, 512], P(('req', 'exp')), may hold values from -0.125 to 0.125
- w_down: bfloat16 [32, 512, 2048], P(('req', 'exp')), may hold values from -0.1875 to 0.1875
Outputs:
- layer_out: bfloat16 [32, 64, 2048], P(('req', 'exp'))
- appended: bfloat16 [32, 512, 2, 2048], P(('req', 'exp'))
The draws below stay inside these ranges and needn't reach their ends.
Inputs may be any that keep to these rules, and one draw needn't show every extreme that they name: `expert_ids`: among the tokens of one request, no expert is named by more than 40 rows.
All inputs are finite; a program needn't handle non-finite values.
Results may differ from the reference program's by a relative error of at most 0.0095.
Values may be sent and summed in bfloat16 or wider, within the bound.
No kernel may reach another device: no remote copies, remote signals or barrier semaphores. Data moves between devices by JAX's collectives and lax.ppermute only.
A program may use at most 128 MiB of HBM per device.

```python
import math
import jax
import jax.numpy as jnp
import numpy as np
from jax import lax

D = 2048
HEADS = 16
HEAD_DIM = 128
FF = 1024
TOP = 8
GROUP = 64
CACHE = 512
REQS = 32
EXPERTS = 16
HALF = 512
CAP = 40


def cache_planes(key):
    key_plane = jax.random.normal(jax.random.fold_in(key, 11), (REQS, CACHE, D), jnp.float32)
    value_plane = jax.random.normal(jax.random.fold_in(key, 12), (REQS, CACHE, D), jnp.float32)
    nudged = jax.random.normal(jax.random.fold_in(key, 13), (REQS, D), jnp.float32)
    key_plane = key_plane.at[:, 1, :].set(key_plane[:, 0, :] + 0.15 * nudged)
    return (key_plane, value_plane)


def draw_cache(key, part):
    key_plane, value_plane = cache_planes(key)
    return jnp.stack([key_plane, value_plane], axis=2).astype(jnp.bfloat16)


def draw_queries(key, part):
    query_plane = jax.random.normal(jax.random.fold_in(key, 21), (REQS, GROUP, D), jnp.float32)
    return query_plane.astype(jnp.bfloat16)


def draw_lengths(key, part):
    spread = jax.random.randint(jax.random.fold_in(key, 31), (REQS,), 8, CACHE - GROUP + 1)
    shuffled = jax.random.permutation(jax.random.fold_in(key, 32), REQS)
    spread = jnp.where(shuffled == 0, CACHE - GROUP, spread)
    spread = jnp.where(shuffled == 1, 8, spread)
    return spread.astype(jnp.int32)


def steps_of(rng, extent, pieces, least, largest):
    factor_of, own = 1.0, jax.random.fold_in(rng, 6)
    for axis_at, blocks in pieces:
        heights = jnp.exp(jax.random.uniform(jax.random.fold_in(own, axis_at), (blocks,), jnp.float32, least / len(pieces), largest / len(pieces)))
        factor_of = factor_of * jnp.repeat(heights, extent[axis_at] // blocks).reshape([-1 if axis == axis_at else 1 for axis in range(len(extent))])
    return factor_of


def assign_block(key, own, number, rows, amount, top, bound, lean):
    order = jax.random.permutation(key, amount)
    crowded, common = load_shares(amount, rows * top, bound, lean, True), load_shares(amount, rows * top, bound, lean, False)
    places = jnp.arange(amount)

    def named(sizes, rotation):
        used = int((sizes > 0).sum())
        fixed = max(1, used // 4)
        moved = fixed + (places - fixed + rotation * (used - fixed)) % max(1, amount - fixed)
        return jnp.zeros((amount,), jnp.int32).at[order[jnp.where(places < fixed, places, moved)]].set(jnp.asarray(sizes, jnp.int32))

    sizes = jnp.where(number % 4 == 0, named(crowded, number // 4), named(common, number - number // 4 - 1))
    mixed = jax.random.permutation(jax.random.fold_in(own, 3), amount)
    donor, taker = mixed[0:amount // 2 * 2:2], mixed[1:amount // 2 * 2:2]
    room = jnp.minimum(sizes[donor] - 1, bound - sizes[taker]) // 2
    room = jnp.where((donor == order[0]) | (taker == order[0]) | (sizes[taker] == 0), 0, jnp.maximum(room, 0))
    moved = jax.random.randint(jax.random.fold_in(own, 4), (amount // 2,), 0, 1 << 20) % (room + 1)
    sizes = sizes.at[donor].add(-moved).at[taker].add(moved)
    members = jnp.searchsorted(jnp.cumsum(sizes), jnp.arange(rows * top), side="right").astype(jnp.int32)
    grid = members.reshape(top, rows).T
    grid = grid[jax.random.permutation(jax.random.fold_in(own, 1), rows)]
    rotation = jax.random.randint(jax.random.fold_in(own, 2), (rows, 1), 0, top)
    return jnp.take_along_axis(grid, (jnp.arange(top)[None, :] + rotation) % top, axis=1)


def load_shares(count, total, most, lean, full):
    loads = [(1 << 20) // math.isqrt(standing ** lean) + 1 for standing in range(1, count + 1)]
    largest = most if full else min(most, max(-(-total // count), total * loads[0] // sum(loads)))
    least = 1 if total - largest >= count - 1 else 0
    given, spare = [largest] + [least] * (count - 1), total - largest - least * (count - 1)
    while spare > 0:
        movable = [i for i in range(1, count) if given[i] < largest] or [i for i in range(1, count) if given[i] < most]
        pool, budget = sum([loads[i] for i in movable]), spare
        for i in movable:
            more = min(most - given[i], max(1, budget * loads[i] // pool), spare)
            given[i] = given[i] + more
            spare = spare - more
    return np.array(given)


def centred(key, extent, deviation, bound, cuts=(), kind=jnp.bfloat16):
    drawn = deviation * jax.random.normal(key, extent, jnp.float32)
    if cuts:
        drawn = drawn * steps_of(key, extent, cuts, -0.22, 0.18)
    return jnp.clip(drawn, -bound, bound).astype(kind)


def setup_inputs(seed: int = 0) -> dict:
    streams_of = jax.random.split(jax.random.key(seed), 13)
    queries = draw_queries(jax.random.fold_in(streams_of[12], 71), 0)
    new_kv = centred(streams_of[1], (REQS, GROUP, 2, D), 1.0, 6.0, ((0, 32),))
    cache = draw_cache(jax.random.fold_in(streams_of[12], 71), 0)
    lengths = draw_lengths(jax.random.fold_in(streams_of[12], 71), 0)
    residual = centred(streams_of[4], (REQS, GROUP, D), 1.0, 6.0, ((0, 32),))
    out_weight = centred(streams_of[5], (D, D), D ** -0.5, 0.125)
    norm_gain = jnp.clip(1.0 + 0.18 * jax.random.normal(streams_of[6], (D,), jnp.float32), 0.1, 1.9)
    expert_ids_keys = jax.random.split(jax.random.fold_in(streams_of[7], 1), REQS * GROUP // GROUP)
    expert_ids_turns = jax.random.permutation(jax.random.fold_in(streams_of[7], 3), REQS * GROUP // GROUP)
    expert_ids = jax.vmap(lambda own, number: assign_block(jax.random.fold_in(streams_of[7], 2), own, number, GROUP, EXPERTS, TOP, CAP, 1))(expert_ids_keys, expert_ids_turns).reshape((REQS, GROUP, TOP))
    gates = jnp.clip(0.1 + 0.9 * jax.random.uniform(streams_of[8], (REQS, GROUP, TOP), jnp.float32) ** steps_of(streams_of[8], (REQS, GROUP, TOP), ((0, 32),), -0.2, 0.2), 0.1, 1.0)
    w_gate = centred(streams_of[9], (2 * EXPERTS, D, HALF), D ** -0.5, 0.125, ((0, 32),))
    w_up = centred(streams_of[10], (2 * EXPERTS, D, HALF), D ** -0.5, 0.125, ((0, 32),))
    w_down = centred(streams_of[11], (2 * EXPERTS, HALF, D), FF ** -0.5, 0.1875, ((0, 32),))
    return dict(queries=queries, new_kv=new_kv, cache=cache, lengths=lengths, residual=residual, out_weight=out_weight, norm_gain=norm_gain, expert_ids=expert_ids, gates=gates, w_gate=w_gate, w_up=w_up, w_down=w_down)


masked_value = -1e+30

def attend_request(query_rows, new_rows, cache_rows, length_now, residual_rows, out_weight):
    key_rows = jnp.concatenate([cache_rows[:, 0], new_rows[:, 0]], axis=0)
    value_rows = jnp.concatenate([cache_rows[:, 1], new_rows[:, 1]], axis=0)
    positions = key_rows.shape[0]
    queried = query_rows.reshape(GROUP, HEADS, HEAD_DIM).astype(jnp.float32)
    keyed = key_rows.reshape(positions, HEADS, HEAD_DIM).astype(jnp.float32)
    valued = value_rows.reshape(positions, HEADS, HEAD_DIM).astype(jnp.float32)
    scores = jnp.einsum('qhd,khd->hqk', queried, keyed) * HEAD_DIM ** (-0.5)
    slot_place = jnp.arange(positions, dtype=jnp.int32)
    counted = (slot_place < length_now) | (slot_place >= CACHE)
    scores = jnp.where(counted[None, None, :], scores, masked_value)
    peak_score = lax.optimization_barrier(jnp.max(scores, axis=-1, keepdims=True))
    raised = jnp.exp(scores - peak_score)
    softmax_bf = (raised / lax.optimization_barrier(jnp.sum(raised, axis=-1, keepdims=True))).astype(jnp.bfloat16)
    mixed_heads = jnp.einsum('hqk,khd->qhd', softmax_bf.astype(jnp.float32), valued)
    attention = mixed_heads.reshape(GROUP, HEADS * HEAD_DIM).astype(jnp.bfloat16)
    stream = residual_rows.astype(jnp.float32) + jnp.dot(attention, out_weight, preferred_element_type=jnp.float32)
    start_at = length_now.astype(jnp.int32)
    appended = lax.dynamic_update_slice(cache_rows, new_rows, (start_at, jnp.int32(0), jnp.int32(0)))
    return (stream, appended)

def reference(queries, new_kv, cache, lengths, residual, out_weight, norm_gain, expert_ids, gates, w_gate, w_up, w_down):

    def per_request(packed):
        return attend_request(packed[0], packed[1], packed[2], packed[3], packed[4], out_weight)
    stream, appended = lax.map(per_request, (queries, new_kv, cache, lengths, residual))
    mean_square = lax.optimization_barrier(jnp.mean(stream * stream, axis=-1, keepdims=True))
    normed = (stream * lax.rsqrt(mean_square + 1e-06) * norm_gain).astype(jnp.bfloat16)
    flat_rows = jnp.concatenate([normed.reshape(REQS * GROUP, D), jnp.zeros((1, D), jnp.bfloat16)], axis=0)
    routed = expert_ids.reshape(REQS, GROUP * TOP)
    weights_flat = gates.reshape(-1)
    row_token = jnp.arange(REQS * GROUP * TOP, dtype=jnp.int32) // TOP
    block_base = jnp.arange(REQS, dtype=jnp.int32)[:, None] * CAP

    def expert_step(accumulated, expert):
        hit_mask = (routed == expert).astype(jnp.int32)
        ranking = jnp.cumsum(hit_mask, axis=1) - hit_mask
        slot_index = jnp.where(hit_mask == 1, block_base + ranking, REQS * CAP).reshape(-1)
        token_of = jnp.full((REQS * CAP,), REQS * GROUP, jnp.int32).at[slot_index].set(row_token, mode='drop')
        gate_of = jnp.zeros((REQS * CAP,), weights_flat.dtype).at[slot_index].set(weights_flat, mode='drop')
        picked_rows = flat_rows[token_of]
        gate_full = jnp.concatenate([w_gate[2 * expert], w_gate[2 * expert + 1]], axis=1)
        up_full = jnp.concatenate([w_up[2 * expert], w_up[2 * expert + 1]], axis=1)
        down_full = jnp.concatenate([w_down[2 * expert], w_down[2 * expert + 1]], axis=0)
        gate_act = jnp.dot(picked_rows, gate_full, preferred_element_type=jnp.float32)
        up_act = jnp.dot(picked_rows, up_full, preferred_element_type=jnp.float32)
        hidden = (jax.nn.silu(gate_act) * up_act).astype(jnp.bfloat16)
        expert_out = jnp.dot(hidden, down_full, preferred_element_type=jnp.float32).astype(jnp.bfloat16)
        accumulated = accumulated.at[token_of].add(gate_of[:, None] * expert_out.astype(accumulated.dtype), mode='drop')
        return (accumulated, None)
    start_sum = jnp.zeros((REQS * GROUP, D), stream.dtype)
    blended, _ = lax.scan(expert_step, start_sum, jnp.arange(EXPERTS, dtype=jnp.int32))
    layer_out = (stream.reshape(REQS * GROUP, D) + blended).astype(jnp.bfloat16).reshape(REQS, GROUP, D)
    return (layer_out, appended)
```

```python
import functools

import jax
import jax.numpy as jnp
from jax import lax
from jax.experimental import pallas as pl
from jax.experimental.pallas import tpu as pltpu
from jax.sharding import Mesh, PartitionSpec as P

HEADS = 16
HEAD_DIM = 128
masked_value = -1e30
ALL = ("req", "chip", "core")
VMEM = pltpu.VMEM


def dot(a, b):
    return jnp.dot(a, b, preferred_element_type=jnp.float32)


def slot_weights(weights, base, mine, chips, capacity):
    tokens, experts = weights.shape
    routed = weights > 0.0
    earlier = lax.broadcasted_iota(jnp.int32, (tokens, tokens), 0) > lax.broadcasted_iota(
        jnp.int32, (tokens, tokens), 1
    )
    ranks = dot(earlier.astype(jnp.bfloat16), routed.astype(jnp.bfloat16))
    ranks = jnp.where(routed, ranks, -1.0)
    expert_at = lax.broadcasted_iota(jnp.int32, (tokens, experts), 1)
    column = lax.broadcasted_iota(jnp.int32, (tokens, chips * capacity), 1)
    gate_at = jnp.zeros((tokens, chips * capacity), jnp.float32)
    hit = jnp.zeros((tokens, chips * capacity), jnp.float32)
    for j in range(chips):
        chosen = expert_at == base + jnp.bitwise_xor(mine, j)
        gate_j = jnp.sum(jnp.where(chosen, weights, 0.0), axis=1, keepdims=True)
        rank_j = jnp.sum(jnp.where(chosen, ranks, 0.0), axis=1, keepdims=True).astype(jnp.int32)
        here = (column == rank_j + j * capacity) & (rank_j >= 0)
        gate_at = jnp.where(here, gate_j, gate_at)
        hit = jnp.where(here, 1.0, hit)
    return gate_at, hit


def gather_rows(rows, weights, base, mine, chips, capacity, outs):
    _, hit = slot_weights(weights, base, mine, chips, capacity)
    picked = lax.dot_general(
        hit.astype(jnp.bfloat16), rows, (((0,), (0,)), ((), ())), preferred_element_type=jnp.float32
    )
    scatter_out(picked, capacity, outs)


def scatter_out(rows, capacity, outs):
    if len(outs) == 1:
        outs[0][...] = rows.astype(outs[0].dtype)
    else:
        for j, out in enumerate(outs):
            out[...] = rows[j * capacity : (j + 1) * capacity].astype(out.dtype)


def stacked(refs):
    if len(refs) == 1:
        return refs[0][...]
    return jnp.concatenate([ref[...].astype(jnp.float32) for ref in refs], axis=0).astype(jnp.bfloat16)


def combined(refs, weights, base, mine, chips, capacity):
    gate_at, _ = slot_weights(weights, base, mine, chips, capacity)
    high = gate_at.astype(jnp.bfloat16)
    low = (gate_at - high.astype(jnp.float32)).astype(jnp.bfloat16)
    tokens = gate_at.shape[0]
    both = dot(jnp.concatenate([high, low], axis=0), stacked(refs))
    return both[:tokens] + both[tokens:]


def attention_kernel(
    chips, capacity, place, length, queries, new_kv, cache, residual, out_weight, gain, weights,
    stream, normed, appended, *rest,
):
    outs, scratch = rest[:-9], rest[-9:]
    cached, newest, queried, resid, projection, keys, values, mixed, sems = scratch
    slots = cache.shape[0]
    group = new_kv.shape[0]
    pieces = 4
    part = slots // pieces
    loads = [
        pltpu.make_async_copy(
            cache.at[pl.ds(i * part, part)], cached.at[pl.ds(i * part, part)], sems.at[i]
        )
        for i in range(pieces)
    ]
    load_new = pltpu.make_async_copy(new_kv, newest, sems.at[pieces])
    load_queries = pltpu.make_async_copy(queries, queried, sems.at[pieces + 1])
    load_resid = pltpu.make_async_copy(residual, resid, sems.at[pieces + 2])
    load_projection = pltpu.make_async_copy(out_weight, projection, sems.at[pieces + 3])
    load_new.start()
    for load in loads:
        load.start()
    load_queries.start()
    load_resid.start()
    load_projection.start()

    def split(source, first, target):
        planes = jnp.swapaxes(source[pl.ds(first, 16)], 0, 1)
        keys[pl.ds(target, 16), :] = planes[0]
        values[pl.ds(target, 16), :] = planes[1]

    load_new.wait()
    for i in range(group // 16):
        split(newest, i * 16, slots + i * 16)
    for i in range(pieces):
        loads[i].wait()

        def step(k, carry):
            first = pl.multiple_of(i * part + k * 16, 16)
            split(cached, first, first)
            return carry

        lax.fori_loop(0, part // 16, step, 0)
    store_cache = pltpu.make_async_copy(cached, appended, sems.at[pieces + 4])
    store_cache.start()
    load_queries.wait()
    positions = slots + group
    slot_place = lax.broadcasted_iota(jnp.int32, (1, positions), 1)
    counted = (slot_place < length[0]) | (slot_place >= slots)
    for h in range(HEADS):
        head = slice(h * HEAD_DIM, (h + 1) * HEAD_DIM)
        scores = lax.dot_general(
            queried[:, head], keys[:, head], (((1,), (1,)), ((), ())), preferred_element_type=jnp.float32
        ) * HEAD_DIM ** (-0.5)
        scores = jnp.where(counted, scores, masked_value)
        raised = jnp.exp(scores - jnp.max(scores, axis=-1, keepdims=True))
        softmax_bf = (raised / jnp.sum(raised, axis=-1, keepdims=True)).astype(jnp.bfloat16)
        mixed[:, head] = dot(softmax_bf, values[:, head]).astype(jnp.bfloat16)
    store_cache.wait()
    store_new = pltpu.make_async_copy(newest, appended.at[pl.ds(length[0], group)], sems.at[pieces + 4])
    store_new.start()
    load_resid.wait()
    load_projection.wait()
    total = resid[...].astype(jnp.float32) + dot(mixed[...], projection[...])
    stream[...] = total
    mean_square = jnp.mean(total * total, axis=-1, keepdims=True)
    rows = (total * lax.rsqrt(mean_square + 1e-06) * gain[...]).astype(jnp.bfloat16)
    normed[...] = rows
    gather_rows(rows, weights[...], place[0], place[1], chips, capacity, outs)
    store_new.wait()


def gather_kernel(chips, capacity, place, rows, weights, *outs):
    gather_rows(rows[...], weights[...], place[0], place[1], chips, capacity, outs)


def expert_kernel(capacity, counts, *refs):
    ins, halves, outs = refs[:counts], refs[counts : counts + 6], refs[counts + 6 :]
    rows = stacked(ins)
    total = None
    for i in range(2):
        gate_half, up_half, down_half = halves[3 * i : 3 * i + 3]
        gate_act = dot(rows, gate_half[...])
        hidden = (gate_act / (1.0 + jnp.exp(-gate_act)) * dot(rows, up_half[...])).astype(jnp.bfloat16)
        partial = dot(hidden, down_half[...])
        total = partial if total is None else total + partial
    scatter_out(total, capacity, outs)


def combine_kernel(chips, capacity, place, weights, *refs):
    refs[-1][...] = combined(refs[:-1], weights[...], place[0], place[1], chips, capacity).astype(jnp.bfloat16)


def final_kernel(chips, capacity, counts, place, weights, stream, *refs):
    total = combined(refs[:counts], weights[...], place[0], place[1], chips, capacity)
    for ref in refs[counts:-1]:
        total = total + ref[...].astype(jnp.float32)
    refs[-1][...] = (stream[...] + total).astype(jnp.bfloat16)


def in_vmem(count):
    return [pl.BlockSpec(memory_space=VMEM)] * count


SMEM_SPEC = pl.BlockSpec(memory_space=pltpu.SMEM)
ANY_SPEC = pl.BlockSpec(memory_space=pl.ANY)


def shards(
    queries, new_kv, cache, lengths, residual, out_weight, norm_gain, expert_ids, gates, w_gate, w_up, w_down,
):
    planes, chips, cores = (lax.axis_size(axis) for axis in ALL)
    mine = lax.axis_index("chip")
    base = lax.axis_index("req") * chips
    experts = planes * chips
    group, features = queries.shape[1:]
    slots = cache.shape[1]
    top_k = expert_ids.shape[2]
    capacity = 5 * group * top_k // (4 * experts)
    tiled = capacity % 8 == 0
    bf16 = jnp.bfloat16
    place = jnp.stack([base, mine]).astype(jnp.int32)

    def params(mib):
        return pltpu.CompilerParams(vmem_limit_bytes=mib << 20)

    def across(x, axis, j):
        size = lax.axis_size(axis)
        return lax.ppermute(x, axis, [(i, i ^ j) for i in range(size)])

    def to_chips(blocks):
        return [blocks[0]] + [across(blocks[j], "chip", j) for j in range(1, chips)]

    if tiled:
        block_shapes = [jax.ShapeDtypeStruct((capacity, features), bf16)] * chips
    else:
        block_shapes = [jax.ShapeDtypeStruct((chips * capacity, features), bf16)]
    blocks_n = len(block_shapes)

    def cut(blocks):
        return blocks if tiled else [blocks[0][j * capacity : (j + 1) * capacity] for j in range(chips)]

    def joined(blocks):
        return blocks if tiled else [jnp.concatenate(blocks, axis=0)]

    own_halves = [w_gate[0], w_up[0], w_down[0]]
    other_halves = [across(half, "core", 1) for half in own_halves]

    weights = jnp.sum(
        jnp.where(
            expert_ids[0][:, :, None] == jnp.arange(experts, dtype=jnp.int32), gates[0][:, :, None], 0.0
        ),
        axis=1,
    )
    weights_of = [weights] + [across(weights, "req", s) for s in range(1, planes)]

    stream, normed, appended, *outgoing = pl.pallas_call(
        functools.partial(attention_kernel, chips, capacity),
        out_shape=[
            jax.ShapeDtypeStruct((group, features), jnp.float32),
            jax.ShapeDtypeStruct((group, features), bf16),
            jax.ShapeDtypeStruct(cache.shape[1:], cache.dtype),
        ]
        + block_shapes,
        in_specs=[SMEM_SPEC, SMEM_SPEC] + [ANY_SPEC] * 5 + in_vmem(2),
        out_specs=in_vmem(2) + [ANY_SPEC] + in_vmem(blocks_n),
        scratch_shapes=[
            VMEM(cache.shape[1:], bf16),
            VMEM(new_kv.shape[1:], bf16),
            VMEM((group, features), bf16),
            VMEM((group, features), bf16),
            VMEM(out_weight.shape, bf16),
            VMEM((slots + group, features), bf16),
            VMEM((slots + group, features), bf16),
            VMEM((group, features), bf16),
            pltpu.SemaphoreType.DMA((9,)),
        ],
        compiler_params=params(40),
        name="attention",
    )(place, lengths, queries[0], new_kv[0], cache[0], residual[0], out_weight, norm_gain[None], weights)

    rows_of = [normed] + [across(normed, "req", s) for s in range(1, planes)]
    partials = []
    for s in range(planes):
        if s > 0:
            outgoing = pl.pallas_call(
                functools.partial(gather_kernel, chips, capacity),
                out_shape=block_shapes,
                in_specs=[SMEM_SPEC] + in_vmem(2),
                out_specs=in_vmem(blocks_n),
                compiler_params=params(16),
                name="gather",
            )(place, rows_of[s], weights_of[s])
        arrived = joined(to_chips(cut(outgoing)))
        results = pl.pallas_call(
            functools.partial(expert_kernel, capacity, blocks_n),
            out_shape=block_shapes,
            in_specs=in_vmem(blocks_n + 6),
            out_specs=in_vmem(blocks_n),
            compiler_params=params(24),
            cost_estimate=pl.CostEstimate(
                flops=12 * chips * capacity * features * w_gate.shape[2],
                bytes_accessed=12 * features * w_gate.shape[2],
                transcendentals=0,
            ),
            name="experts",
        )(*arrived, *own_halves, *other_halves)
        returned = joined(to_chips(cut(results)))
        if s == 0:
            own_returned = returned
        else:
            partial = pl.pallas_call(
                functools.partial(combine_kernel, chips, capacity),
                out_shape=jax.ShapeDtypeStruct((group, features), bf16),
                in_specs=[SMEM_SPEC] + in_vmem(1 + blocks_n),
                out_specs=pl.BlockSpec(memory_space=VMEM),
                compiler_params=params(16),
                name="combine",
            )(place, weights_of[s], *returned)
            partials.append(across(partial, "req", s))
    layer_out = pl.pallas_call(
        functools.partial(final_kernel, chips, capacity, blocks_n),
        out_shape=jax.ShapeDtypeStruct((group, features), bf16),
        in_specs=[SMEM_SPEC] + in_vmem(2 + blocks_n + len(partials)),
        out_specs=pl.BlockSpec(memory_space=VMEM),
        compiler_params=params(16),
        name="final",
    )(place, weights, stream, *own_returned, *partials)
    return (layer_out[None], appended[None])


def solution(mesh):
    planes, width = (mesh.shape[axis] for axis in ("req", "exp"))
    split = Mesh(mesh.devices.reshape(planes, width // 2, 2), ALL)
    by_device = P(ALL)
    placed = (by_device,) * 5 + (P(), P()) + (by_device,) * 5
    return jax.shard_map(
        shards,
        mesh=split,
        in_specs=placed,
        out_specs=(by_device, by_device),
        check_vma=False,
    )
```

```python
import functools

import jax
import jax.numpy as jnp
from jax import lax
from jax.experimental import pallas as pl
from jax.experimental.pallas import tpu as pltpu
from jax.sharding import Mesh, PartitionSpec as P

HEADS = 16
HEAD_DIM = 128
masked_value = -1e30
ALL = ("req", "chip", "core")
VMEM = pltpu.VMEM


def dot(a, b):
    return jnp.dot(a, b, preferred_element_type=jnp.float32)


def slot_weights(weights, base, mine, chips, capacity):
    tokens, experts = weights.shape
    routed = weights > 0.0
    earlier = lax.broadcasted_iota(jnp.int32, (tokens, tokens), 0) > lax.broadcasted_iota(
        jnp.int32, (tokens, tokens), 1
    )
    ranks = dot(earlier.astype(jnp.bfloat16), routed.astype(jnp.bfloat16))
    ranks = jnp.where(routed, ranks, -1.0)
    expert_at = lax.broadcasted_iota(jnp.int32, (tokens, experts), 1)
    column = lax.broadcasted_iota(jnp.int32, (tokens, chips * capacity), 1)
    gate_at = jnp.zeros((tokens, chips * capacity), jnp.float32)
    hit = jnp.zeros((tokens, chips * capacity), jnp.float32)
    for j in range(chips):
        chosen = expert_at == base + jnp.bitwise_xor(mine, j)
        gate_j = jnp.sum(jnp.where(chosen, weights, 0.0), axis=1, keepdims=True)
        rank_j = jnp.sum(jnp.where(chosen, ranks, 0.0), axis=1, keepdims=True).astype(jnp.int32)
        here = (column == rank_j + j * capacity) & (rank_j >= 0)
        gate_at = jnp.where(here, gate_j, gate_at)
        hit = jnp.where(here, 1.0, hit)
    return gate_at, hit


def routing(ids, gates, experts):
    top_k, tokens = ids.shape
    expert_at = lax.broadcasted_iota(jnp.int32, (experts, tokens), 0)
    found = jnp.zeros((experts, tokens), jnp.float32)
    for k in range(top_k):
        found = jnp.where(ids[k : k + 1, :] == expert_at, gates[k : k + 1, :], found)
    return found.T


def position(chips):
    return lax.axis_index("req") * chips, lax.axis_index("chip")


def unpacked(payload, features, experts):
    high = payload[:, features : features + experts].astype(jnp.float32)
    low = payload[:, features + experts : features + 2 * experts].astype(jnp.float32)
    return high + low


def gather_rows(rows, weights, chips, capacity, outs):
    base, mine = position(chips)
    _, hit = slot_weights(weights, base, mine, chips, capacity)
    picked = lax.dot_general(
        hit.astype(jnp.bfloat16), rows, (((0,), (0,)), ((), ())), preferred_element_type=jnp.float32
    )
    scatter_out(picked, capacity, outs)


def scatter_out(rows, capacity, outs):
    if len(outs) == 1:
        outs[0][...] = rows.astype(outs[0].dtype)
    else:
        for j, out in enumerate(outs):
            out[...] = rows[j * capacity : (j + 1) * capacity].astype(out.dtype)


def stacked(refs):
    if len(refs) == 1:
        return refs[0][...]
    return jnp.concatenate([ref[...].astype(jnp.float32) for ref in refs], axis=0).astype(jnp.bfloat16)


def combined(refs, weights, chips, capacity):
    base, mine = position(chips)
    gate_at, _ = slot_weights(weights, base, mine, chips, capacity)
    high = gate_at.astype(jnp.bfloat16)
    low = (gate_at - high.astype(jnp.float32)).astype(jnp.bfloat16)
    tokens = gate_at.shape[0]
    both = dot(jnp.concatenate([high, low], axis=0), stacked(refs))
    return both[:tokens] + both[tokens:]


def attention_kernel(
    chips, capacity, experts, length, queries, new_kv, cache, residual, out_weight, gain, ids, gates,
    stream, payload, appended, *rest,
):
    outs, scratch = rest[:-9], rest[-9:]
    cached, newest, queried, resid, projection, keys, values, mixed, sems = scratch
    slots = cache.shape[0]
    group = new_kv.shape[0]
    pieces = 4
    part = slots // pieces
    loads = [
        pltpu.make_async_copy(
            cache.at[pl.ds(i * part, part)], cached.at[pl.ds(i * part, part)], sems.at[i]
        )
        for i in range(pieces)
    ]
    load_new = pltpu.make_async_copy(new_kv, newest, sems.at[pieces])
    load_queries = pltpu.make_async_copy(queries, queried, sems.at[pieces + 1])
    load_resid = pltpu.make_async_copy(residual, resid, sems.at[pieces + 2])
    load_projection = pltpu.make_async_copy(out_weight, projection, sems.at[pieces + 3])
    load_new.start()
    for load in loads:
        load.start()
    load_queries.start()
    load_resid.start()
    load_projection.start()

    def split(source, first, target):
        planes = jnp.swapaxes(source[pl.ds(first, 16)], 0, 1)
        keys[pl.ds(target, 16), :] = planes[0]
        values[pl.ds(target, 16), :] = planes[1]

    load_new.wait()
    for i in range(group // 16):
        split(newest, i * 16, slots + i * 16)
    for i in range(pieces):
        loads[i].wait()

        def step(k, carry):
            first = pl.multiple_of(i * part + k * 16, 16)
            split(cached, first, first)
            return carry

        lax.fori_loop(0, part // 16, step, 0)
    store_cache = pltpu.make_async_copy(cached, appended, sems.at[pieces + 4])
    store_cache.start()
    load_queries.wait()
    positions = slots + group
    slot_place = lax.broadcasted_iota(jnp.int32, (1, positions), 1)
    counted = (slot_place < length[0]) | (slot_place >= slots)
    for h in range(HEADS):
        head = slice(h * HEAD_DIM, (h + 1) * HEAD_DIM)
        scores = lax.dot_general(
            queried[:, head], keys[:, head], (((1,), (1,)), ((), ())), preferred_element_type=jnp.float32
        ) * HEAD_DIM ** (-0.5)
        scores = jnp.where(counted, scores, masked_value)
        raised = jnp.exp(scores - jnp.max(scores, axis=-1, keepdims=True))
        softmax_bf = (raised / jnp.sum(raised, axis=-1, keepdims=True)).astype(jnp.bfloat16)
        mixed[:, head] = dot(softmax_bf, values[:, head]).astype(jnp.bfloat16)
    store_cache.wait()
    store_new = pltpu.make_async_copy(newest, appended.at[pl.ds(length[0], group)], sems.at[pieces + 4])
    store_new.start()
    load_resid.wait()
    load_projection.wait()
    total = resid[...].astype(jnp.float32) + dot(mixed[...], projection[...])
    stream[...] = total
    mean_square = jnp.mean(total * total, axis=-1, keepdims=True)
    rows = (total * lax.rsqrt(mean_square + 1e-06) * gain[...]).astype(jnp.bfloat16)
    features = rows.shape[1]
    weights = routing(ids[...], gates[...], experts)
    high = weights.astype(jnp.bfloat16)
    low = (weights - high.astype(jnp.float32)).astype(jnp.bfloat16)
    spare = payload.shape[1] - features - 2 * experts
    trail = [high, low] + ([jnp.zeros((rows.shape[0], spare), jnp.bfloat16)] if spare else [])
    payload[:, :features] = rows
    payload[:, features:] = jnp.concatenate(trail, axis=1)
    gather_rows(rows, weights, chips, capacity, outs)
    store_new.wait()


def gather_kernel(chips, capacity, experts, features, payload, *outs):
    weights = unpacked(payload, features, experts)
    gather_rows(payload[:, :features], weights, chips, capacity, outs)


def expert_kernel(capacity, counts, *refs):
    ins, halves, outs = refs[:counts], refs[counts : counts + 6], refs[counts + 6 :]
    rows = stacked(ins)
    total = None
    for i in range(2):
        gate_half, up_half, down_half = halves[3 * i : 3 * i + 3]
        gate_act = dot(rows, gate_half[...])
        hidden = (gate_act / (1.0 + jnp.exp(-gate_act)) * dot(rows, up_half[...])).astype(jnp.bfloat16)
        partial = dot(hidden, down_half[...])
        total = partial if total is None else total + partial
    scatter_out(total, capacity, outs)


def combine_kernel(chips, capacity, experts, features, payload, *refs):
    weights = unpacked(payload, features, experts)
    refs[-1][...] = combined(refs[:-1], weights, chips, capacity).astype(jnp.bfloat16)


def final_kernel(chips, capacity, experts, features, counts, payload, stream, *refs):
    weights = unpacked(payload, features, experts)
    total = combined(refs[:counts], weights, chips, capacity)
    for ref in refs[counts:-1]:
        total = total + ref[...].astype(jnp.float32)
    refs[-1][...] = (stream[...] + total).astype(jnp.bfloat16)


def in_vmem(count):
    return [pl.BlockSpec(memory_space=VMEM)] * count


SMEM_SPEC = pl.BlockSpec(memory_space=pltpu.SMEM)
HBM_SPEC = pl.BlockSpec(memory_space=pltpu.HBM)


def shards(
    queries, new_kv, cache, lengths, residual, out_weight, norm_gain, expert_ids, gates, w_gate, w_up, w_down,
):
    planes, chips, cores = (lax.axis_size(axis) for axis in ALL)
    experts = planes * chips
    group, features = queries.shape[1:]
    slots = cache.shape[1]
    top_k = expert_ids.shape[2]
    capacity = 5 * group * top_k // (4 * experts)
    tiled = capacity % 8 == 0
    bf16 = jnp.bfloat16
    width = features + -(-2 * experts // 128) * 128

    def params(mib):
        return pltpu.CompilerParams(vmem_limit_bytes=mib << 20)

    def across(x, axis, j):
        size = lax.axis_size(axis)
        return lax.ppermute(x, axis, [(i, i ^ j) for i in range(size)])

    def to_chips(blocks):
        return [blocks[0]] + [across(blocks[j], "chip", j) for j in range(1, chips)]

    if tiled:
        block_shapes = [jax.ShapeDtypeStruct((capacity, features), bf16)] * chips
    else:
        block_shapes = [jax.ShapeDtypeStruct((chips * capacity, features), bf16)]
    blocks_n = len(block_shapes)

    def cut(blocks):
        return blocks if tiled else [blocks[0][j * capacity : (j + 1) * capacity] for j in range(chips)]

    def joined(blocks):
        return blocks if tiled else [jnp.concatenate(blocks, axis=0)]

    own_halves = [w_gate[0], w_up[0], w_down[0]]
    other_halves = [across(half, "core", 1) for half in own_halves]
    halves = [pltpu.with_memory_space_constraint(half, VMEM) for half in own_halves + other_halves]

    stream, payload, appended, *outgoing = pl.pallas_call(
        functools.partial(attention_kernel, chips, capacity, experts),
        out_shape=[
            jax.ShapeDtypeStruct((group, features), jnp.float32),
            jax.ShapeDtypeStruct((group, width), bf16),
            jax.ShapeDtypeStruct(cache.shape[1:], cache.dtype),
        ]
        + block_shapes,
        in_specs=[SMEM_SPEC] + [HBM_SPEC] * 5 + in_vmem(3),
        out_specs=in_vmem(2) + [HBM_SPEC] + in_vmem(blocks_n),
        scratch_shapes=[
            VMEM(cache.shape[1:], bf16),
            VMEM(new_kv.shape[1:], bf16),
            VMEM((group, features), bf16),
            VMEM((group, features), bf16),
            VMEM(out_weight.shape, bf16),
            VMEM((slots + group, features), bf16),
            VMEM((slots + group, features), bf16),
            VMEM((group, features), bf16),
            pltpu.SemaphoreType.DMA((9,)),
        ],
        compiler_params=params(24),
        cost_estimate=pl.CostEstimate(
            flops=12_000_000_000, bytes_accessed=24 * features * features // 4, transcendentals=0
        ),
        name="attention",
    )(
        lengths,
        *[
            pltpu.with_memory_space_constraint(x, pltpu.HBM)
            for x in (queries[0], new_kv[0], cache[0], residual[0], out_weight)
        ],
        norm_gain[None],
        expert_ids[0].T,
        gates[0].T,
    )

    payload_of = [payload] + [across(payload, "req", s) for s in range(1, planes)]
    partials = []
    for s in range(planes):
        if s > 0:
            outgoing = pl.pallas_call(
                functools.partial(gather_kernel, chips, capacity, experts, features),
                out_shape=block_shapes,
                in_specs=in_vmem(1),
                out_specs=in_vmem(blocks_n),
                compiler_params=params(8),
                name="gather",
            )(payload_of[s])
        arrived = joined(to_chips(cut(outgoing)))
        results = pl.pallas_call(
            functools.partial(expert_kernel, capacity, blocks_n),
            out_shape=block_shapes,
            in_specs=in_vmem(blocks_n + 6),
            out_specs=in_vmem(blocks_n),
            compiler_params=params(8),
            cost_estimate=pl.CostEstimate(
                flops=12 * chips * capacity * features * w_gate.shape[2],
                bytes_accessed=12 * features * w_gate.shape[2],
                transcendentals=0,
            ),
            name="experts",
        )(*arrived, *halves)
        returned = joined(to_chips(cut(results)))
        if s == 0:
            own_returned = returned
        else:
            partial = pl.pallas_call(
                functools.partial(combine_kernel, chips, capacity, experts, features),
                out_shape=jax.ShapeDtypeStruct((group, features), bf16),
                in_specs=in_vmem(1 + blocks_n),
                out_specs=pl.BlockSpec(memory_space=VMEM),
                compiler_params=params(8),
                name="combine",
            )(payload_of[s], *returned)
            partials.append(across(partial, "req", s))
    layer_out = pl.pallas_call(
        functools.partial(final_kernel, chips, capacity, experts, features, blocks_n),
        out_shape=jax.ShapeDtypeStruct((group, features), bf16),
        in_specs=in_vmem(2 + blocks_n + len(partials)),
        out_specs=pl.BlockSpec(memory_space=VMEM),
        compiler_params=params(8),
        name="final",
    )(payload, stream, *own_returned, *partials)
    return (layer_out[None], appended[None])


def solution(mesh):
    planes, width = (mesh.shape[axis] for axis in ("req", "exp"))
    split = Mesh(mesh.devices.reshape(planes, width // 2, 2), ALL)
    by_device = P(ALL)
    placed = (by_device,) * 5 + (P(), P()) + (by_device,) * 5
    return jax.shard_map(
        shards,
        mesh=split,
        in_specs=placed,
        out_specs=(by_device, by_device),
        check_vma=False,
    )
```

```python
import functools

import jax
import jax.numpy as jnp
from jax import lax
from jax.experimental import pallas as pl
from jax.experimental.pallas import tpu as pltpu
from jax.sharding import Mesh, PartitionSpec as P

HEADS = 16
HEAD_DIM = 128
masked_value = -1e30
ALL = ("req", "chip", "core")
VMEM = pltpu.VMEM


def dot(a, b):
    return jnp.dot(a, b, preferred_element_type=jnp.float32)


def slot_weights(weights, base, mine, chips, capacity):
    tokens, experts = weights.shape
    routed = weights > 0.0
    earlier = lax.broadcasted_iota(jnp.int32, (tokens, tokens), 0) > lax.broadcasted_iota(
        jnp.int32, (tokens, tokens), 1
    )
    ranks = dot(earlier.astype(jnp.bfloat16), routed.astype(jnp.bfloat16))
    ranks = jnp.where(routed, ranks, -1.0)
    expert_at = lax.broadcasted_iota(jnp.int32, (tokens, experts), 1)
    column = lax.broadcasted_iota(jnp.int32, (tokens, chips * capacity), 1)
    gate_at = jnp.zeros((tokens, chips * capacity), jnp.float32)
    hit = jnp.zeros((tokens, chips * capacity), jnp.float32)
    for j in range(chips):
        chosen = expert_at == base + jnp.bitwise_xor(mine, j)
        gate_j = jnp.sum(jnp.where(chosen, weights, 0.0), axis=1, keepdims=True)
        rank_j = jnp.sum(jnp.where(chosen, ranks, 0.0), axis=1, keepdims=True).astype(jnp.int32)
        here = (column == rank_j + j * capacity) & (rank_j >= 0)
        gate_at = jnp.where(here, gate_j, gate_at)
        hit = jnp.where(here, 1.0, hit)
    return gate_at, hit


def routing(ids, gates, experts):
    top_k, tokens = ids.shape
    expert_at = lax.broadcasted_iota(jnp.int32, (experts, tokens), 0)
    found = jnp.zeros((experts, tokens), jnp.float32)
    for k in range(top_k):
        found = jnp.where(ids[k : k + 1, :] == expert_at, gates[k : k + 1, :], found)
    return found.T


def position(chips):
    return lax.axis_index("req") * chips, lax.axis_index("chip")


def unpacked(payload, features, experts):
    high = payload[:, features : features + experts].astype(jnp.float32)
    low = payload[:, features + experts : features + 2 * experts].astype(jnp.float32)
    return high + low


def gather_rows(rows, weights, chips, capacity, outs):
    base, mine = position(chips)
    _, hit = slot_weights(weights, base, mine, chips, capacity)
    picked = lax.dot_general(
        hit.astype(jnp.bfloat16), rows, (((0,), (0,)), ((), ())), preferred_element_type=jnp.float32
    )
    scatter_out(picked, capacity, outs)


def scatter_out(rows, capacity, outs):
    if len(outs) == 1:
        outs[0][...] = rows.astype(outs[0].dtype)
    else:
        for j, out in enumerate(outs):
            out[...] = rows[j * capacity : (j + 1) * capacity].astype(out.dtype)


def stacked(refs):
    if len(refs) == 1:
        return refs[0][...]
    return jnp.concatenate([ref[...].astype(jnp.float32) for ref in refs], axis=0).astype(jnp.bfloat16)


def combined(refs, weights, chips, capacity):
    base, mine = position(chips)
    gate_at, _ = slot_weights(weights, base, mine, chips, capacity)
    high = gate_at.astype(jnp.bfloat16)
    low = (gate_at - high.astype(jnp.float32)).astype(jnp.bfloat16)
    tokens = gate_at.shape[0]
    both = dot(jnp.concatenate([high, low], axis=0), stacked(refs))
    return both[:tokens] + both[tokens:]


def attention_kernel(
    chips, capacity, experts, length, queries, new_kv, cache, residual, out_weight, gain_in, ids_in, gates_in,
    stream, payload, appended, *rest,
):
    outs, scratch = rest[:-12], rest[-12:]
    cached, newest, queried, resid, projection, gain, ids, gates, keys, values, mixed, sems = scratch
    slots = cache.shape[0]
    group = new_kv.shape[0]
    pieces = 4
    part = slots // pieces
    loads = [
        pltpu.make_async_copy(
            cache.at[pl.ds(i * part, part)], cached.at[pl.ds(i * part, part)], sems.at[i]
        )
        for i in range(pieces)
    ]
    load_new = pltpu.make_async_copy(new_kv, newest, sems.at[pieces])
    load_queries = pltpu.make_async_copy(queries, queried, sems.at[pieces + 1])
    load_resid = pltpu.make_async_copy(residual, resid, sems.at[pieces + 2])
    load_projection = pltpu.make_async_copy(out_weight, projection, sems.at[pieces + 3])
    load_small = [
        pltpu.make_async_copy(source, target, sems.at[pieces + 5 + i])
        for i, (source, target) in enumerate([(gain_in, gain), (ids_in, ids), (gates_in, gates)])
    ]
    load_new.start()
    for load in loads:
        load.start()
    load_queries.start()
    load_resid.start()
    load_projection.start()
    for load in load_small:
        load.start()

    def split(source, first, target):
        planes = jnp.swapaxes(source[pl.ds(first, 16)], 0, 1)
        keys[pl.ds(target, 16), :] = planes[0]
        values[pl.ds(target, 16), :] = planes[1]

    load_new.wait()
    for i in range(group // 16):
        split(newest, i * 16, slots + i * 16)
    for i in range(pieces):
        loads[i].wait()

        def step(k, carry):
            first = pl.multiple_of(i * part + k * 16, 16)
            split(cached, first, first)
            return carry

        lax.fori_loop(0, part // 16, step, 0)
    store_cache = pltpu.make_async_copy(cached, appended, sems.at[pieces + 4])
    store_cache.start()
    load_queries.wait()
    positions = slots + group
    slot_place = lax.broadcasted_iota(jnp.int32, (1, positions), 1)
    counted = (slot_place < length[0]) | (slot_place >= slots)
    for h in range(HEADS):
        head = slice(h * HEAD_DIM, (h + 1) * HEAD_DIM)
        scores = lax.dot_general(
            queried[:, head], keys[:, head], (((1,), (1,)), ((), ())), preferred_element_type=jnp.float32
        ) * HEAD_DIM ** (-0.5)
        scores = jnp.where(counted, scores, masked_value)
        raised = jnp.exp(scores - jnp.max(scores, axis=-1, keepdims=True))
        softmax_bf = (raised / jnp.sum(raised, axis=-1, keepdims=True)).astype(jnp.bfloat16)
        mixed[:, head] = dot(softmax_bf, values[:, head]).astype(jnp.bfloat16)
    store_cache.wait()
    store_new = pltpu.make_async_copy(newest, appended.at[pl.ds(length[0], group)], sems.at[pieces + 4])
    store_new.start()
    load_resid.wait()
    load_projection.wait()
    for load in load_small:
        load.wait()
    total = resid[...].astype(jnp.float32) + dot(mixed[...], projection[...])
    stream[...] = total
    mean_square = jnp.mean(total * total, axis=-1, keepdims=True)
    rows = (total * lax.rsqrt(mean_square + 1e-06) * gain[...]).astype(jnp.bfloat16)
    features = rows.shape[1]
    weights = routing(ids[...], gates[...], experts)
    high = weights.astype(jnp.bfloat16)
    low = (weights - high.astype(jnp.float32)).astype(jnp.bfloat16)
    spare = payload.shape[1] - features - 2 * experts
    trail = [high, low] + ([jnp.zeros((rows.shape[0], spare), jnp.bfloat16)] if spare else [])
    payload[:, :features] = rows
    payload[:, features:] = jnp.concatenate(trail, axis=1)
    gather_rows(rows, weights, chips, capacity, outs)
    store_new.wait()


def gather_kernel(chips, capacity, experts, features, payload, *outs):
    weights = unpacked(payload, features, experts)
    gather_rows(payload[:, :features], weights, chips, capacity, outs)


def expert_kernel(capacity, counts, *refs):
    ins, halves, outs = refs[:counts], refs[counts : counts + 6], refs[counts + 6 :]
    rows = stacked(ins)
    total = None
    for i in range(2):
        gate_half, up_half, down_half = halves[3 * i : 3 * i + 3]
        gate_act = dot(rows, gate_half[...])
        hidden = (gate_act / (1.0 + jnp.exp(-gate_act)) * dot(rows, up_half[...])).astype(jnp.bfloat16)
        partial = dot(hidden, down_half[...])
        total = partial if total is None else total + partial
    scatter_out(total, capacity, outs)


def combine_kernel(chips, capacity, experts, features, payload, *refs):
    weights = unpacked(payload, features, experts)
    refs[-1][...] = combined(refs[:-1], weights, chips, capacity).astype(jnp.bfloat16)


def final_kernel(chips, capacity, experts, features, counts, payload, stream, *refs):
    weights = unpacked(payload, features, experts)
    total = combined(refs[:counts], weights, chips, capacity)
    for ref in refs[counts:-1]:
        total = total + ref[...].astype(jnp.float32)
    refs[-1][...] = (stream[...] + total).astype(jnp.bfloat16)


def in_vmem(count):
    return [pl.BlockSpec(memory_space=VMEM)] * count


SMEM_SPEC = pl.BlockSpec(memory_space=pltpu.SMEM)
HBM_SPEC = pl.BlockSpec(memory_space=pltpu.HBM)


Z_FIRST = (1, 2, 3)
ORDER = (("in", 0), ("in", 1), ("out", 0), ("in", 2), ("out", 1), ("in", 3), ("out", 2), ("out", 3))
LAG = 2


def shards(
    queries, new_kv, cache, lengths, residual, out_weight, norm_gain, expert_ids, gates, w_gate, w_up, w_down,
):
    planes, chips, cores = (lax.axis_size(axis) for axis in ALL)
    experts = planes * chips
    group, features = queries.shape[1:]
    slots = cache.shape[1]
    top_k = expert_ids.shape[2]
    capacity = 5 * group * top_k // (4 * experts)
    tiled = capacity % 8 == 0
    bf16 = jnp.bfloat16
    width = features + -(-2 * experts // 128) * 128

    def params(mib):
        return pltpu.CompilerParams(vmem_limit_bytes=mib << 20)

    def across(x, axis, j):
        size = lax.axis_size(axis)
        return lax.ppermute(x, axis, [(i, i ^ j) for i in range(size)])

    def to_chips(blocks):
        return [blocks[0]] + [across(blocks[j], "chip", j) for j in range(1, chips)]

    if tiled:
        block_shapes = [jax.ShapeDtypeStruct((capacity, features), bf16)] * chips
    else:
        block_shapes = [jax.ShapeDtypeStruct((chips * capacity, features), bf16)]
    blocks_n = len(block_shapes)

    def cut(blocks):
        return blocks if tiled else [blocks[0][j * capacity : (j + 1) * capacity] for j in range(chips)]

    def joined(blocks):
        return blocks if tiled else [jnp.concatenate(blocks, axis=0)]

    own_halves = [w_gate[0], w_up[0], w_down[0]]
    other_halves = [across(half, "core", 1) for half in own_halves]

    stream, payload, appended, *outgoing = pl.pallas_call(
        functools.partial(attention_kernel, chips, capacity, experts),
        out_shape=[
            jax.ShapeDtypeStruct((group, features), jnp.float32),
            jax.ShapeDtypeStruct((group, width), bf16),
            jax.ShapeDtypeStruct(cache.shape[1:], cache.dtype),
        ]
        + block_shapes,
        in_specs=[SMEM_SPEC] + [HBM_SPEC] * 8,
        out_specs=in_vmem(2) + [HBM_SPEC] + in_vmem(blocks_n),
        scratch_shapes=[
            VMEM(cache.shape[1:], bf16),
            VMEM(new_kv.shape[1:], bf16),
            VMEM((group, features), bf16),
            VMEM((group, features), bf16),
            VMEM(out_weight.shape, bf16),
            VMEM((1, features), jnp.float32),
            VMEM((top_k, group), jnp.int32),
            VMEM((top_k, group), jnp.float32),
            VMEM((slots + group, features), bf16),
            VMEM((slots + group, features), bf16),
            VMEM((group, features), bf16),
            pltpu.SemaphoreType.DMA((12,)),
        ],
        compiler_params=params(24),
        cost_estimate=pl.CostEstimate(
            flops=12_000_000_000, bytes_accessed=24 * features * features // 4, transcendentals=0
        ),
        name="attention",
    )(
        lengths,
        *[
            pltpu.with_memory_space_constraint(x, pltpu.HBM)
            for x in (
                queries[0], new_kv[0], cache[0], residual[0], out_weight, norm_gain[None], expert_ids[0].T, gates[0].T,
            )
        ],
    )

    payload, outgoing, other_halves = lax.optimization_barrier((payload, outgoing, other_halves))
    halves = [pltpu.with_memory_space_constraint(half, VMEM) for half in own_halves + other_halves]

    def gather(packed):
        return pl.pallas_call(
            functools.partial(gather_kernel, chips, capacity, experts, features),
            out_shape=block_shapes,
            in_specs=in_vmem(1),
            out_specs=in_vmem(blocks_n),
            compiler_params=params(8),
            name="gather",
        )(packed)

    def run_experts(arrived):
        return pl.pallas_call(
            functools.partial(expert_kernel, capacity, blocks_n),
            out_shape=block_shapes,
            in_specs=in_vmem(blocks_n + 6),
            out_specs=in_vmem(blocks_n),
            compiler_params=params(8),
            cost_estimate=pl.CostEstimate(
                flops=12 * chips * capacity * features * w_gate.shape[2],
                bytes_accessed=12 * features * w_gate.shape[2],
                transcendentals=0,
            ),
            name="experts",
        )(*arrived, *halves)

    def combine(packed, returned):
        return pl.pallas_call(
            functools.partial(combine_kernel, chips, capacity, experts, features),
            out_shape=jax.ShapeDtypeStruct((group, features), bf16),
            in_specs=in_vmem(1 + blocks_n),
            out_specs=pl.BlockSpec(memory_space=VMEM),
            compiler_params=params(8),
            name="combine",
        )(packed, *returned)

    payload_of = {0: payload}
    for s in Z_FIRST:
        payload_of[s] = across(payload, "req", s)
    arrived_of, returned_of, partials, moved = {}, {}, [], []
    for k, (way, s) in enumerate(ORDER):
        if way == "in":
            if s not in payload_of:
                later, moved[-1] = lax.optimization_barrier((payload, moved[-1]))
                payload_of[s] = across(later, "req", s)
            blocks = outgoing if s == 0 else gather(payload_of[s])
        else:
            blocks = run_experts(arrived_of[s])
        if k >= LAG:
            blocks, moved[k - LAG] = lax.optimization_barrier((blocks, moved[k - LAG]))
            pw, ps = ORDER[k - LAG]
            (arrived_of if pw == "in" else returned_of)[ps] = moved[k - LAG]
        got = joined(to_chips(cut(blocks)))
        moved.append(got)
        (arrived_of if way == "in" else returned_of)[s] = got
        if way == "out" and s > 0:
            partials.append(across(combine(payload_of[s], got), "req", s))
    own_returned = returned_of[0]
    layer_out = pl.pallas_call(
        functools.partial(final_kernel, chips, capacity, experts, features, blocks_n),
        out_shape=jax.ShapeDtypeStruct((group, features), bf16),
        in_specs=in_vmem(2 + blocks_n + len(partials)),
        out_specs=pl.BlockSpec(memory_space=VMEM),
        compiler_params=params(8),
        name="final",
    )(payload, stream, *own_returned, *partials)
    return (layer_out[None], appended[None])


def solution(mesh):
    planes, width = (mesh.shape[axis] for axis in ("req", "exp"))
    split = Mesh(mesh.devices.reshape(planes, width // 2, 2), ALL)
    by_device = P(ALL)
    placed = (by_device,) * 5 + (P(), P()) + (by_device,) * 5
    return jax.shard_map(
        shards,
        mesh=split,
        in_specs=placed,
        out_specs=(by_device, by_device),
        check_vma=False,
    )
```

```python
import functools

import jax
import jax.numpy as jnp
from jax import lax
from jax.experimental import pallas as pl
from jax.experimental.pallas import tpu as pltpu
from jax.sharding import Mesh, PartitionSpec as P

HEADS = 16
HEAD_DIM = 128
masked_value = -1e30
ALL = ("req", "chip", "core")
VMEM = pltpu.VMEM
HEAD_PARTS = 2


def dot(a, b):
    return jnp.dot(a, b, preferred_element_type=jnp.float32)


def slot_weights(weights, base, mine, chips, capacity):
    tokens, experts = weights.shape
    routed = weights > 0.0
    earlier = lax.broadcasted_iota(jnp.int32, (tokens, tokens), 0) > lax.broadcasted_iota(
        jnp.int32, (tokens, tokens), 1
    )
    ranks = dot(earlier.astype(jnp.bfloat16), routed.astype(jnp.bfloat16))
    ranks = jnp.where(routed, ranks, -1.0)
    expert_at = lax.broadcasted_iota(jnp.int32, (tokens, experts), 1)
    column = lax.broadcasted_iota(jnp.int32, (tokens, chips * capacity), 1)
    gate_at = jnp.zeros((tokens, chips * capacity), jnp.float32)
    hit = jnp.zeros((tokens, chips * capacity), jnp.float32)
    for j in range(chips):
        chosen = expert_at == base + jnp.bitwise_xor(mine, j)
        gate_j = jnp.sum(jnp.where(chosen, weights, 0.0), axis=1, keepdims=True)
        rank_j = jnp.sum(jnp.where(chosen, ranks, 0.0), axis=1, keepdims=True).astype(jnp.int32)
        here = (column == rank_j + j * capacity) & (rank_j >= 0)
        gate_at = jnp.where(here, gate_j, gate_at)
        hit = jnp.where(here, 1.0, hit)
    return gate_at, hit


def routing(ids, gates, experts):
    top_k, tokens = ids.shape
    expert_at = lax.broadcasted_iota(jnp.int32, (experts, tokens), 0)
    found = jnp.zeros((experts, tokens), jnp.float32)
    for k in range(top_k):
        found = jnp.where(ids[k : k + 1, :] == expert_at, gates[k : k + 1, :], found)
    return found.T


def position(chips):
    return lax.axis_index("req") * chips, lax.axis_index("chip")


def unpacked(payload, features, experts):
    high = payload[:, features : features + experts].astype(jnp.float32)
    low = payload[:, features + experts : features + 2 * experts].astype(jnp.float32)
    return high + low


def gather_rows(rows, weights, chips, capacity, outs):
    base, mine = position(chips)
    _, hit = slot_weights(weights, base, mine, chips, capacity)
    picked = lax.dot_general(
        hit.astype(jnp.bfloat16), rows, (((0,), (0,)), ((), ())), preferred_element_type=jnp.float32
    )
    scatter_out(picked, capacity, outs)


def scatter_out(rows, capacity, outs):
    if len(outs) == 1:
        outs[0][...] = rows.astype(outs[0].dtype)
    else:
        for j, out in enumerate(outs):
            out[...] = rows[j * capacity : (j + 1) * capacity].astype(out.dtype)


def stacked(refs):
    if len(refs) == 1:
        return refs[0][...]
    return jnp.concatenate([ref[...].astype(jnp.float32) for ref in refs], axis=0).astype(jnp.bfloat16)


def combined(refs, weights, chips, capacity):
    base, mine = position(chips)
    gate_at, _ = slot_weights(weights, base, mine, chips, capacity)
    high = gate_at.astype(jnp.bfloat16)
    low = (gate_at - high.astype(jnp.float32)).astype(jnp.bfloat16)
    tokens = gate_at.shape[0]
    both = dot(jnp.concatenate([high, low], axis=0), stacked(refs))
    return both[:tokens] + both[tokens:]


def attention_kernel(
    chips, capacity, experts, length, queries, new_kv, cache, residual, out_weight, gain_in, ids_in, gates_in,
    stream, payload, cached, newest, *rest,
):
    outs, scratch = rest[:-10], rest[-10:]
    queried, resid, projection, gain, ids, gates, keys, values, mixed, sems = scratch
    slots = cache.shape[0]
    group, features = queries.shape
    parts = HEAD_PARTS
    wide = features // parts
    small = [(ids_in, ids), (gates_in, gates), (gain_in, gain)]
    first = [(new_kv, newest), (queries, queried)]
    spans = [pl.ds(i * wide, wide) for i in range(parts)]
    pairs = small + first + [(cache.at[:, :, span], cached.at[:, :, span]) for span in spans]
    pairs += [(residual, resid)] + [(out_weight.at[span], projection.at[span]) for span in spans]
    loads = [pltpu.make_async_copy(source, target, sems.at[i]) for i, (source, target) in enumerate(pairs)]
    for load in loads:
        load.start()
    load_small, load_first, load_cache = loads[:3], loads[3:5], loads[5 : 5 + parts]
    load_resid, load_projection = loads[5 + parts], loads[6 + parts :]

    def split(source, start, target, span):
        both = jnp.swapaxes(source[pl.ds(start, 16), :, span], 0, 1)
        keys[pl.ds(target, 16), span] = both[0]
        values[pl.ds(target, 16), span] = both[1]

    for load in load_small:
        load.wait()
    weights = routing(ids[...], gates[...], experts)
    high = weights.astype(jnp.bfloat16)
    low = (weights - high.astype(jnp.float32)).astype(jnp.bfloat16)
    spare = payload.shape[1] - features - 2 * experts
    trail = [high, low] + ([jnp.zeros((group, spare), jnp.bfloat16)] if spare else [])
    payload[:, features:] = jnp.concatenate(trail, axis=1)
    for load in load_first:
        load.wait()
    for i in range(group // 16):
        split(newest, i * 16, slots + i * 16, slice(None))
    positions = slots + group
    slot_place = lax.broadcasted_iota(jnp.int32, (1, positions), 1)
    counted = (slot_place < length[0]) | (slot_place >= slots)
    heads_part = HEADS // parts
    for part in range(parts):
        load_cache[part].wait()
        span = slice(part * wide, (part + 1) * wide)

        def step(k, carry):
            start = pl.multiple_of(k * 16, 16)
            split(cached, start, start, span)
            return carry

        lax.fori_loop(0, slots // 16, step, 0, unroll=4)
        heads = [slice(h * HEAD_DIM, (h + 1) * HEAD_DIM) for h in range(part * heads_part, (part + 1) * heads_part)]
        scores = jnp.concatenate(
            [
                lax.dot_general(
                    queried[:, head], keys[:, head], (((1,), (1,)), ((), ())), preferred_element_type=jnp.float32
                )
                for head in heads
            ],
            axis=0,
        ) * HEAD_DIM ** (-0.5)
        scores = jnp.where(counted, scores, masked_value)
        raised = jnp.exp(scores - jnp.max(scores, axis=-1, keepdims=True))
        softmax_bf = (raised / jnp.sum(raised, axis=-1, keepdims=True)).astype(jnp.bfloat16)
        for i, head in enumerate(heads):
            mixed[:, head] = dot(softmax_bf[i * group : (i + 1) * group], values[:, head]).astype(jnp.bfloat16)
    load_resid.wait()
    total = resid[...].astype(jnp.float32)
    for part in range(parts):
        load_projection[part].wait()
        span = slice(part * wide, (part + 1) * wide)
        total = total + dot(mixed[:, span], projection[span, :])
    stream[...] = total
    mean_square = jnp.mean(total * total, axis=-1, keepdims=True)
    rows = (total * lax.rsqrt(mean_square + 1e-06) * gain[...]).astype(jnp.bfloat16)
    payload[:, :features] = rows
    gather_rows(rows, weights, chips, capacity, outs)


def gather_kernel(chips, capacity, experts, features, payload, *outs):
    weights = unpacked(payload, features, experts)
    gather_rows(payload[:, :features], weights, chips, capacity, outs)


def expert_kernel(capacity, counts, span, length, cached, newest, *refs):
    if span is None or span[0] > 0:
        refs = refs[1:]
    ins, halves, outs = refs[:counts], refs[counts : counts + 6], refs[counts + 6 : -2]
    appended, sem = refs[-2:]
    if span is None:
        write = pltpu.make_async_copy(newest, appended.at[pl.ds(length[0], newest.shape[0])], sem)
    else:
        piece = pl.ds(span[0], span[1] - span[0])
        write = pltpu.make_async_copy(cached.at[piece], appended.at[piece], sem)
    write.start()
    rows = stacked(ins)
    total = None
    for i in range(2):
        gate_half, up_half, down_half = halves[3 * i : 3 * i + 3]
        gate_act = dot(rows, gate_half[...])
        hidden = (gate_act / (1.0 + jnp.exp(-gate_act)) * dot(rows, up_half[...])).astype(jnp.bfloat16)
        partial = dot(hidden, down_half[...])
        total = partial if total is None else total + partial
    scatter_out(total, capacity, outs)
    write.wait()


def combine_kernel(chips, capacity, experts, features, payload, *refs):
    weights = unpacked(payload, features, experts)
    refs[-1][...] = combined(refs[:-1], weights, chips, capacity).astype(jnp.bfloat16)


def own_kernel(chips, capacity, experts, features, payload, stream, *refs):
    weights = unpacked(payload, features, experts)
    refs[-1][...] = stream[...] + combined(refs[:-1], weights, chips, capacity)


def in_vmem(count):
    return [pl.BlockSpec(memory_space=VMEM)] * count


SMEM_SPEC = pl.BlockSpec(memory_space=pltpu.SMEM)
HBM_SPEC = pl.BlockSpec(memory_space=pltpu.HBM)


Z_FIRST = (1, 2, 3)
ORDER = (("in", 0), ("in", 1), ("out", 0), ("in", 2), ("out", 1), ("in", 3), ("out", 2), ("out", 3))
LAG = 2


def shards(
    queries, new_kv, cache, lengths, residual, out_weight, norm_gain, expert_ids, gates, w_gate, w_up, w_down,
):
    planes, chips, cores = (lax.axis_size(axis) for axis in ALL)
    experts = planes * chips
    group, features = queries.shape[1:]
    slots = cache.shape[1]
    top_k = expert_ids.shape[2]
    capacity = 5 * group * top_k // (4 * experts)
    tiled = capacity % 8 == 0
    bf16 = jnp.bfloat16
    width = features + -(-2 * experts // 128) * 128

    def params(mib):
        return pltpu.CompilerParams(vmem_limit_bytes=mib << 20)

    def across(x, axis, j):
        size = lax.axis_size(axis)
        return lax.ppermute(x, axis, [(i, i ^ j) for i in range(size)])

    def to_chips(blocks):
        return [blocks[0]] + [across(blocks[j], "chip", j) for j in range(1, chips)]

    if tiled:
        block_shapes = [jax.ShapeDtypeStruct((capacity, features), bf16)] * chips
    else:
        block_shapes = [jax.ShapeDtypeStruct((chips * capacity, features), bf16)]
    blocks_n = len(block_shapes)

    def cut(blocks):
        return blocks if tiled else [blocks[0][j * capacity : (j + 1) * capacity] for j in range(chips)]

    def joined(blocks):
        return blocks if tiled else [jnp.concatenate(blocks, axis=0)]

    own_halves = [w_gate[0], w_up[0], w_down[0]]
    other_halves = [across(half, "core", 1) for half in own_halves]

    stream, payload, cached, newest, *outgoing = pl.pallas_call(
        functools.partial(attention_kernel, chips, capacity, experts),
        out_shape=[
            jax.ShapeDtypeStruct((group, features), jnp.float32),
            jax.ShapeDtypeStruct((group, width), bf16),
            jax.ShapeDtypeStruct(cache.shape[1:], bf16),
            jax.ShapeDtypeStruct(new_kv.shape[1:], bf16),
        ]
        + block_shapes,
        in_specs=[SMEM_SPEC] + [HBM_SPEC] * 8,
        out_specs=in_vmem(4 + blocks_n),
        scratch_shapes=[
            VMEM((group, features), bf16),
            VMEM((group, features), bf16),
            VMEM(out_weight.shape, bf16),
            VMEM((1, features), jnp.float32),
            VMEM((top_k, group), jnp.int32),
            VMEM((top_k, group), jnp.float32),
            VMEM((slots + group, features), bf16),
            VMEM((slots + group, features), bf16),
            VMEM((group, features), bf16),
            pltpu.SemaphoreType.DMA((6 + 2 * HEAD_PARTS,)),
        ],
        compiler_params=params(24),
        cost_estimate=pl.CostEstimate(
            flops=12_000_000_000, bytes_accessed=24 * features * features // 4, transcendentals=0
        ),
        name="attention",
    )(
        lengths,
        *[
            pltpu.with_memory_space_constraint(x, pltpu.HBM)
            for x in (
                queries[0], new_kv[0], cache[0], residual[0], out_weight, norm_gain[None], expert_ids[0].T, gates[0].T,
            )
        ],
    )

    payload, outgoing, other_halves = lax.optimization_barrier((payload, outgoing, other_halves))
    halves = [pltpu.with_memory_space_constraint(half, VMEM) for half in own_halves + other_halves]

    def gather(packed):
        return pl.pallas_call(
            functools.partial(gather_kernel, chips, capacity, experts, features),
            out_shape=block_shapes,
            in_specs=in_vmem(1),
            out_specs=in_vmem(blocks_n),
            compiler_params=params(8),
            name="gather",
        )(packed)

    held = [pltpu.with_memory_space_constraint(x, VMEM) for x in (cached, newest)]
    cuts = [slots * i // (planes - 1) for i in range(planes)]
    spans = list(zip(cuts[:-1], cuts[1:])) + [None]

    def run_experts(arrived, call, appended):
        before = [] if call == 0 else [pltpu.with_memory_space_constraint(appended, pltpu.HBM)]
        *results, appended = pl.pallas_call(
            functools.partial(expert_kernel, capacity, blocks_n, spans[call]),
            out_shape=block_shapes + [jax.ShapeDtypeStruct(cache.shape[1:], cache.dtype)],
            in_specs=[SMEM_SPEC] + in_vmem(2) + [HBM_SPEC] * len(before) + in_vmem(blocks_n + 6),
            out_specs=in_vmem(blocks_n) + [HBM_SPEC],
            scratch_shapes=[pltpu.SemaphoreType.DMA],
            input_output_aliases={3: blocks_n} if before else {},
            compiler_params=params(8),
            cost_estimate=pl.CostEstimate(
                flops=12 * chips * capacity * features * w_gate.shape[2],
                bytes_accessed=12 * features * w_gate.shape[2],
                transcendentals=0,
            ),
            name="experts",
        )(lengths, *held, *before, *arrived, *halves)
        return results, appended

    def combine(packed, returned):
        return pl.pallas_call(
            functools.partial(combine_kernel, chips, capacity, experts, features),
            out_shape=jax.ShapeDtypeStruct((group, features), bf16),
            in_specs=in_vmem(1 + blocks_n),
            out_specs=pl.BlockSpec(memory_space=VMEM),
            compiler_params=params(8),
            name="combine",
        )(packed, *returned)

    payload_of = {0: payload}
    calls, appended = 0, None
    for s in Z_FIRST:
        payload_of[s] = across(payload, "req", s)
    arrived_of, returned_of, partials, moved, due = {}, {}, [], [], []
    for k, (way, s) in enumerate(ORDER):
        if way == "in":
            if s not in payload_of:
                later, moved[-1] = lax.optimization_barrier((payload, moved[-1]))
                payload_of[s] = across(later, "req", s)
            blocks = outgoing if s == 0 else gather(payload_of[s])
        else:
            blocks, appended = run_experts(arrived_of[s], calls, appended)
            calls += 1
        if k >= LAG:
            pw, ps = ORDER[k - LAG]
            if pw == "out" and ps > 0:
                partial = combine(payload_of[ps], moved[k - LAG])
                blocks, partial = lax.optimization_barrier((blocks, partial))
                due.append(({1: 7, 2: 99, 3: 99}[ps], len(partials)))
                partials.append(across(partial, "req", ps))
                returned_of.pop(ps)
            else:
                blocks, moved[k - LAG] = lax.optimization_barrier((blocks, moved[k - LAG]))
                (arrived_of if pw == "in" else returned_of)[ps] = moved[k - LAG]
        while due and due[0][0] <= k:
            at = due.pop(0)[1]
            blocks, partials[at] = lax.optimization_barrier((blocks, partials[at]))
        got = joined(to_chips(cut(blocks)))
        moved.append(got)
        (arrived_of if way == "in" else returned_of)[s] = got
    for s in sorted(returned_of):
        if s > 0:
            partials.append(across(combine(payload_of[s], returned_of[s]), "req", s))
    own_returned = returned_of[0]
    total = pl.pallas_call(
        functools.partial(own_kernel, chips, capacity, experts, features),
        out_shape=jax.ShapeDtypeStruct((group, features), jnp.float32),
        in_specs=in_vmem(2 + blocks_n),
        out_specs=pl.BlockSpec(memory_space=VMEM),
        compiler_params=params(8),
        name="own",
    )(payload, stream, *own_returned)
    for partial in partials:
        total = total + partial.astype(jnp.float32)
    layer_out = total.astype(bf16)
    return (layer_out[None], appended[None])


def solution(mesh):
    planes, width = (mesh.shape[axis] for axis in ("req", "exp"))
    split = Mesh(mesh.devices.reshape(planes, width // 2, 2), ALL)
    by_device = P(ALL)
    placed = (by_device,) * 5 + (P(), P()) + (by_device,) * 5
    return jax.shard_map(
        shards,
        mesh=split,
        in_specs=placed,
        out_specs=(by_device, by_device),
        check_vma=False,
    )
```

```python
import functools

import jax
import jax.numpy as jnp
from jax import lax
from jax.experimental import pallas as pl
from jax.experimental.pallas import tpu as pltpu
from jax.sharding import Mesh, PartitionSpec as P

HEADS = 16
HEAD_DIM = 128
masked_value = -1e30
ALL = ("req", "chip", "core")
VMEM = pltpu.VMEM
HEAD_PARTS = 2


def dot(a, b):
    return jnp.dot(a, b, preferred_element_type=jnp.float32)


def slot_weights(weights, base, mine, chips, capacity):
    tokens, experts = weights.shape
    routed = weights > 0.0
    earlier = lax.broadcasted_iota(jnp.int32, (tokens, tokens), 0) > lax.broadcasted_iota(
        jnp.int32, (tokens, tokens), 1
    )
    ranks = dot(earlier.astype(jnp.bfloat16), routed.astype(jnp.bfloat16))
    ranks = jnp.where(routed, ranks, -1.0)
    expert_at = lax.broadcasted_iota(jnp.int32, (tokens, experts), 1)
    column = lax.broadcasted_iota(jnp.int32, (tokens, chips * capacity), 1)
    gate_at = jnp.zeros((tokens, chips * capacity), jnp.float32)
    hit = jnp.zeros((tokens, chips * capacity), jnp.float32)
    for j in range(chips):
        chosen = expert_at == base + jnp.bitwise_xor(mine, j)
        gate_j = jnp.sum(jnp.where(chosen, weights, 0.0), axis=1, keepdims=True)
        rank_j = jnp.sum(jnp.where(chosen, ranks, 0.0), axis=1, keepdims=True).astype(jnp.int32)
        here = (column == rank_j + j * capacity) & (rank_j >= 0)
        gate_at = jnp.where(here, gate_j, gate_at)
        hit = jnp.where(here, 1.0, hit)
    return gate_at, hit


def routing(ids, gates, experts):
    top_k, tokens = ids.shape
    expert_at = lax.broadcasted_iota(jnp.int32, (experts, tokens), 0)
    found = jnp.zeros((experts, tokens), jnp.float32)
    for k in range(top_k):
        found = jnp.where(ids[k : k + 1, :] == expert_at, gates[k : k + 1, :], found)
    return found.T


def position(chips):
    return lax.axis_index("req") * chips, lax.axis_index("chip")


def unpacked(payload, features, experts):
    high = payload[:, features : features + experts].astype(jnp.float32)
    low = payload[:, features + experts : features + 2 * experts].astype(jnp.float32)
    return high + low


def gather_rows(rows, weights, chips, capacity, outs):
    base, mine = position(chips)
    _, hit = slot_weights(weights, base, mine, chips, capacity)
    picked = lax.dot_general(
        hit.astype(jnp.bfloat16), rows, (((0,), (0,)), ((), ())), preferred_element_type=jnp.float32
    )
    scatter_out(picked, capacity, outs)


def scatter_out(rows, capacity, outs):
    if len(outs) == 1:
        outs[0][...] = rows.astype(outs[0].dtype)
    else:
        for j, out in enumerate(outs):
            out[...] = rows[j * capacity : (j + 1) * capacity].astype(out.dtype)


def stacked(refs):
    if len(refs) == 1:
        return refs[0][...]
    return jnp.concatenate([ref[...].astype(jnp.float32) for ref in refs], axis=0).astype(jnp.bfloat16)


def combined(refs, weights, chips, capacity):
    base, mine = position(chips)
    gate_at, _ = slot_weights(weights, base, mine, chips, capacity)
    high = gate_at.astype(jnp.bfloat16)
    low = (gate_at - high.astype(jnp.float32)).astype(jnp.bfloat16)
    tokens = gate_at.shape[0]
    both = dot(jnp.concatenate([high, low], axis=0), stacked(refs))
    return both[:tokens] + both[tokens:]


def attention_kernel(
    chips, capacity, experts, length, queries, new_kv, cache, residual, out_weight, gain_in, ids_in, gates_in,
    stream, payload, cached, newest, *rest,
):
    outs, scratch = rest[:-10], rest[-10:]
    queried, resid, projection, gain, ids, gates, keys, values, mixed, sems = scratch
    slots = cache.shape[0]
    group, features = queries.shape
    parts = HEAD_PARTS
    wide = features // parts
    small = [(ids_in, ids), (gates_in, gates), (gain_in, gain)]
    first = [(new_kv, newest), (queries, queried)]
    spans = [pl.ds(i * wide, wide) for i in range(parts)]
    pairs = small + first + [(cache.at[:, :, span], cached.at[:, :, span]) for span in spans]
    pairs += [(residual, resid)] + [(out_weight.at[span], projection.at[span]) for span in spans]
    loads = [pltpu.make_async_copy(source, target, sems.at[i]) for i, (source, target) in enumerate(pairs)]
    for load in loads:
        load.start()
    load_small, load_first, load_cache = loads[:3], loads[3:5], loads[5 : 5 + parts]
    load_resid, load_projection = loads[5 + parts], loads[6 + parts :]

    def split(source, start, target, span):
        both = jnp.swapaxes(source[pl.ds(start, 16), :, span], 0, 1)
        keys[pl.ds(target, 16), span] = both[0]
        values[pl.ds(target, 16), span] = both[1]

    for load in load_small:
        load.wait()
    weights = routing(ids[...], gates[...], experts)
    high = weights.astype(jnp.bfloat16)
    low = (weights - high.astype(jnp.float32)).astype(jnp.bfloat16)
    spare = payload.shape[1] - features - 2 * experts
    trail = [high, low] + ([jnp.zeros((group, spare), jnp.bfloat16)] if spare else [])
    payload[:, features:] = jnp.concatenate(trail, axis=1)
    for load in load_first:
        load.wait()
    for i in range(group // 16):
        split(newest, i * 16, slots + i * 16, slice(None))
    positions = slots + group
    slot_place = lax.broadcasted_iota(jnp.int32, (1, positions), 1)
    counted = (slot_place < length[0]) | (slot_place >= slots)
    heads_part = HEADS // parts
    for part in range(parts):
        load_cache[part].wait()
        span = slice(part * wide, (part + 1) * wide)

        def step(k, carry):
            start = pl.multiple_of(k * 16, 16)
            split(cached, start, start, span)
            return carry

        lax.fori_loop(0, slots // 16, step, 0, unroll=4)
        heads = [slice(h * HEAD_DIM, (h + 1) * HEAD_DIM) for h in range(part * heads_part, (part + 1) * heads_part)]
        scores = jnp.concatenate(
            [
                lax.dot_general(
                    queried[:, head], keys[:, head], (((1,), (1,)), ((), ())), preferred_element_type=jnp.float32
                )
                for head in heads
            ],
            axis=0,
        ) * HEAD_DIM ** (-0.5)
        scores = jnp.where(counted, scores, masked_value)
        raised = jnp.exp(scores - jnp.max(scores, axis=-1, keepdims=True))
        softmax_bf = (raised / jnp.sum(raised, axis=-1, keepdims=True)).astype(jnp.bfloat16)
        for i, head in enumerate(heads):
            mixed[:, head] = dot(softmax_bf[i * group : (i + 1) * group], values[:, head]).astype(jnp.bfloat16)
    load_resid.wait()
    total = resid[...].astype(jnp.float32)
    for part in range(parts):
        load_projection[part].wait()
        span = slice(part * wide, (part + 1) * wide)
        total = total + dot(mixed[:, span], projection[span, :])
    stream[...] = total
    mean_square = jnp.mean(total * total, axis=-1, keepdims=True)
    rows = (total * lax.rsqrt(mean_square + 1e-06) * gain[...]).astype(jnp.bfloat16)
    payload[:, :features] = rows
    gather_rows(rows, weights, chips, capacity, outs)


def gather_kernel(chips, capacity, experts, features, payload, *outs):
    weights = unpacked(payload, features, experts)
    gather_rows(payload[:, :features], weights, chips, capacity, outs)


def expert_kernel(capacity, counts, span, length, cached, newest, *refs):
    if span is None or span[0] > 0:
        refs = refs[1:]
    ins, halves, outs = refs[:counts], refs[counts : counts + 6], refs[counts + 6 : -2]
    appended, sem = refs[-2:]
    if span is None:
        write = pltpu.make_async_copy(newest, appended.at[pl.ds(length[0], newest.shape[0])], sem)
    else:
        piece = pl.ds(span[0], span[1] - span[0])
        write = pltpu.make_async_copy(cached.at[piece], appended.at[piece], sem)
    write.start()
    rows = stacked(ins)
    total = None
    for i in range(2):
        gate_half, up_half, down_half = halves[3 * i : 3 * i + 3]
        gate_act = dot(rows, gate_half[...])
        hidden = (gate_act / (1.0 + jnp.exp(-gate_act)) * dot(rows, up_half[...])).astype(jnp.bfloat16)
        partial = dot(hidden, down_half[...])
        total = partial if total is None else total + partial
    scatter_out(total, capacity, outs)
    write.wait()


def combine_kernel(chips, capacity, experts, features, counts, payload, *refs):
    weights = unpacked(payload, features, experts)
    total = combined(refs[:counts], weights, chips, capacity)
    for ref in refs[counts:-1]:
        total = total + ref[...].astype(jnp.float32)
    refs[-1][...] = total.astype(jnp.bfloat16)


def own_kernel(chips, capacity, experts, features, payload, stream, *refs):
    weights = unpacked(payload, features, experts)
    refs[-1][...] = stream[...] + combined(refs[:-1], weights, chips, capacity)


def in_vmem(count):
    return [pl.BlockSpec(memory_space=VMEM)] * count


SMEM_SPEC = pl.BlockSpec(memory_space=pltpu.SMEM)
HBM_SPEC = pl.BlockSpec(memory_space=pltpu.HBM)


ORDER = (("in", 0), ("out", 0), ("in", 3), ("in", 1), ("out", 3), ("in", 2), ("out", 2), ("out", 1))
LAG = 2
DUE = {}


def shards(
    queries, new_kv, cache, lengths, residual, out_weight, norm_gain, expert_ids, gates, w_gate, w_up, w_down,
):
    planes, chips, cores = (lax.axis_size(axis) for axis in ALL)
    experts = planes * chips
    group, features = queries.shape[1:]
    slots = cache.shape[1]
    top_k = expert_ids.shape[2]
    capacity = 5 * group * top_k // (4 * experts)
    tiled = capacity % 8 == 0
    bf16 = jnp.bfloat16
    width = features + -(-2 * experts // 128) * 128

    def params(mib):
        return pltpu.CompilerParams(vmem_limit_bytes=mib << 20)

    def across(x, axis, j):
        size = lax.axis_size(axis)
        return lax.ppermute(x, axis, [(i, i ^ j) for i in range(size)])

    def to_chips(blocks):
        return [blocks[0]] + [across(blocks[j], "chip", j) for j in range(1, chips)]

    if tiled:
        block_shapes = [jax.ShapeDtypeStruct((capacity, features), bf16)] * chips
    else:
        block_shapes = [jax.ShapeDtypeStruct((chips * capacity, features), bf16)]
    blocks_n = len(block_shapes)

    def cut(blocks):
        return blocks if tiled else [blocks[0][j * capacity : (j + 1) * capacity] for j in range(chips)]

    def joined(blocks):
        return blocks if tiled else [jnp.concatenate(blocks, axis=0)]

    own_halves = [w_gate[0], w_up[0], w_down[0]]
    other_halves = [across(half, "core", 1) for half in own_halves]

    stream, payload, cached, newest, *outgoing = pl.pallas_call(
        functools.partial(attention_kernel, chips, capacity, experts),
        out_shape=[
            jax.ShapeDtypeStruct((group, features), jnp.float32),
            jax.ShapeDtypeStruct((group, width), bf16),
            jax.ShapeDtypeStruct(cache.shape[1:], bf16),
            jax.ShapeDtypeStruct(new_kv.shape[1:], bf16),
        ]
        + block_shapes,
        in_specs=[SMEM_SPEC] + [HBM_SPEC] * 8,
        out_specs=in_vmem(4 + blocks_n),
        scratch_shapes=[
            VMEM((group, features), bf16),
            VMEM((group, features), bf16),
            VMEM(out_weight.shape, bf16),
            VMEM((1, features), jnp.float32),
            VMEM((top_k, group), jnp.int32),
            VMEM((top_k, group), jnp.float32),
            VMEM((slots + group, features), bf16),
            VMEM((slots + group, features), bf16),
            VMEM((group, features), bf16),
            pltpu.SemaphoreType.DMA((6 + 2 * HEAD_PARTS,)),
        ],
        compiler_params=params(24),
        cost_estimate=pl.CostEstimate(
            flops=12_000_000_000, bytes_accessed=24 * features * features // 4, transcendentals=0
        ),
        name="attention",
    )(
        lengths,
        *[
            pltpu.with_memory_space_constraint(x, pltpu.HBM)
            for x in (
                queries[0], new_kv[0], cache[0], residual[0], out_weight, norm_gain[None], expert_ids[0].T, gates[0].T,
            )
        ],
    )

    payload, outgoing, other_halves = lax.optimization_barrier((payload, outgoing, other_halves))
    halves = [pltpu.with_memory_space_constraint(half, VMEM) for half in own_halves + other_halves]

    def gather(packed):
        return pl.pallas_call(
            functools.partial(gather_kernel, chips, capacity, experts, features),
            out_shape=block_shapes,
            in_specs=in_vmem(1),
            out_specs=in_vmem(blocks_n),
            compiler_params=params(8),
            name="gather",
        )(packed)

    held = [pltpu.with_memory_space_constraint(x, VMEM) for x in (cached, newest)]
    cuts = [slots * i // (planes - 1) for i in range(planes)]
    spans = list(zip(cuts[:-1], cuts[1:])) + [None]

    def run_experts(arrived, call, appended):
        before = [] if call == 0 else [pltpu.with_memory_space_constraint(appended, pltpu.HBM)]
        *results, appended = pl.pallas_call(
            functools.partial(expert_kernel, capacity, blocks_n, spans[call]),
            out_shape=block_shapes + [jax.ShapeDtypeStruct(cache.shape[1:], cache.dtype)],
            in_specs=[SMEM_SPEC] + in_vmem(2) + [HBM_SPEC] * len(before) + in_vmem(blocks_n + 6),
            out_specs=in_vmem(blocks_n) + [HBM_SPEC],
            scratch_shapes=[pltpu.SemaphoreType.DMA],
            input_output_aliases={3: blocks_n} if before else {},
            compiler_params=params(8),
            cost_estimate=pl.CostEstimate(
                flops=12 * chips * capacity * features * w_gate.shape[2],
                bytes_accessed=12 * features * w_gate.shape[2],
                transcendentals=0,
            ),
            name="experts",
        )(lengths, *held, *before, *arrived, *halves)
        return results, appended

    def combine(packed, returned, extra):
        return pl.pallas_call(
            functools.partial(combine_kernel, chips, capacity, experts, features, blocks_n),
            out_shape=jax.ShapeDtypeStruct((group, features), bf16),
            in_specs=in_vmem(1 + blocks_n + len(extra)),
            out_specs=pl.BlockSpec(memory_space=VMEM),
            compiler_params=params(8),
            name="combine",
        )(packed, *returned, *extra)

    payload_of = {0: payload, 1: across(payload, "req", 1), 3: across(payload, "req", 3)}
    payload_of[2] = across(payload_of[3], "req", 1)
    calls, appended = 0, None
    arrived_of, returned_of, partials, moved = {}, {}, {}, []

    def send_back(s, hold):
        extra = [partials.pop(3)] if s == 2 else []
        partial = combine(payload_of[s], returned_of.pop(s), extra)
        hold, partial = lax.optimization_barrier((hold, partial))
        partials[s] = across(partial, "req", 2 if s == 2 else 1)
        return hold

    for k, (way, s) in enumerate(ORDER):
        if way == "in":
            blocks = outgoing if s == 0 else gather(payload_of[s])
        else:
            blocks, appended = run_experts(arrived_of[s], calls, appended)
            calls += 1
        if k >= LAG:
            pw, ps = ORDER[k - LAG]
            if pw == "out" and ps > 0:
                blocks = send_back(ps, blocks)
            else:
                blocks, got = lax.optimization_barrier((blocks, moved[k - LAG]))
                (arrived_of if pw == "in" else returned_of)[ps] = got
        if k in DUE:
            blocks, partials[DUE[k]] = lax.optimization_barrier((blocks, partials[DUE[k]]))
        got = joined(to_chips(cut(blocks)))
        moved.append(got)
        (arrived_of if way == "in" else returned_of)[s] = got
    for way, s in ORDER:
        if way == "out" and s > 0 and s in returned_of:
            send_back(s, ())
    own_returned = returned_of[0]
    total = pl.pallas_call(
        functools.partial(own_kernel, chips, capacity, experts, features),
        out_shape=jax.ShapeDtypeStruct((group, features), jnp.float32),
        in_specs=in_vmem(2 + blocks_n),
        out_specs=pl.BlockSpec(memory_space=VMEM),
        compiler_params=params(8),
        name="own",
    )(payload, stream, *own_returned)
    for partial in partials.values():
        total = total + partial.astype(jnp.float32)
    layer_out = total.astype(bf16)
    return (layer_out[None], appended[None])


def solution(mesh):
    planes, width = (mesh.shape[axis] for axis in ("req", "exp"))
    split = Mesh(mesh.devices.reshape(planes, width // 2, 2), ALL)
    by_device = P(ALL)
    placed = (by_device,) * 5 + (P(), P()) + (by_device,) * 5
    return jax.shard_map(
        shards,
        mesh=split,
        in_specs=placed,
        out_specs=(by_device, by_device),
        check_vma=False,
    )
```

```python
import functools

import jax
import jax.numpy as jnp
from jax import lax
from jax.experimental import pallas as pl
from jax.experimental.pallas import tpu as pltpu
from jax.sharding import Mesh, PartitionSpec as P

HEADS = 16
HEAD_DIM = 128
masked_value = -1e30
ALL = ("req", "chip", "core")
VMEM = pltpu.VMEM
HEAD_PARTS = 2


def dot(a, b):
    return jnp.dot(a, b, preferred_element_type=jnp.float32)


def slot_weights(weights, base, mine, chips, capacity):
    tokens, experts = weights.shape
    routed = weights > 0.0
    earlier = lax.broadcasted_iota(jnp.int32, (tokens, tokens), 0) > lax.broadcasted_iota(
        jnp.int32, (tokens, tokens), 1
    )
    ranks = dot(earlier.astype(jnp.bfloat16), routed.astype(jnp.bfloat16))
    ranks = jnp.where(routed, ranks, -1.0)
    expert_at = lax.broadcasted_iota(jnp.int32, (tokens, experts), 1)
    column = lax.broadcasted_iota(jnp.int32, (tokens, chips * capacity), 1)
    gate_at = jnp.zeros((tokens, chips * capacity), jnp.float32)
    hit = jnp.zeros((tokens, chips * capacity), jnp.float32)
    for j in range(chips):
        chosen = expert_at == base + jnp.bitwise_xor(mine, j)
        gate_j = jnp.sum(jnp.where(chosen, weights, 0.0), axis=1, keepdims=True)
        rank_j = jnp.sum(jnp.where(chosen, ranks, 0.0), axis=1, keepdims=True).astype(jnp.int32)
        here = (column == rank_j + j * capacity) & (rank_j >= 0)
        gate_at = jnp.where(here, gate_j, gate_at)
        hit = jnp.where(here, 1.0, hit)
    return gate_at, hit


def routing(ids, gates, experts):
    top_k, tokens = ids.shape
    expert_at = lax.broadcasted_iota(jnp.int32, (experts, tokens), 0)
    found = jnp.zeros((experts, tokens), jnp.float32)
    for k in range(top_k):
        found = jnp.where(ids[k : k + 1, :] == expert_at, gates[k : k + 1, :], found)
    return found.T


def position(chips):
    return lax.axis_index("req") * chips, lax.axis_index("chip")


def unpacked(payload, features, experts):
    high = payload[:, features : features + experts].astype(jnp.float32)
    low = payload[:, features + experts : features + 2 * experts].astype(jnp.float32)
    return high + low


def gather_rows(rows, weights, chips, capacity, outs):
    base, mine = position(chips)
    gate_at, hit = slot_weights(weights, base, mine, chips, capacity)
    high = gate_at.astype(jnp.bfloat16)
    low = (gate_at - high.astype(jnp.float32)).astype(jnp.bfloat16)
    outs[0][...] = jnp.concatenate([high, low], axis=0)
    picked = lax.dot_general(
        hit.astype(jnp.bfloat16), rows, (((0,), (0,)), ((), ())), preferred_element_type=jnp.float32
    )
    scatter_out(picked, capacity, outs[1:])


def scatter_out(rows, capacity, outs):
    if len(outs) == 1:
        outs[0][...] = rows.astype(outs[0].dtype)
    else:
        for j, out in enumerate(outs):
            out[...] = rows[j * capacity : (j + 1) * capacity].astype(out.dtype)


def stacked(refs):
    if len(refs) == 1:
        return refs[0][...]
    return jnp.concatenate([ref[...].astype(jnp.float32) for ref in refs], axis=0).astype(jnp.bfloat16)


def combined(refs, table):
    both = dot(table[...], stacked(refs))
    tokens = both.shape[0] // 2
    return both[:tokens] + both[tokens:]


def attention_kernel(
    chips, capacity, experts, length, queries, new_kv, cache, residual, out_weight, gain_in, ids_in, gates_in,
    stream, payload, cached, newest, *rest,
):
    outs, scratch = rest[:-10], rest[-10:]
    queried, resid, projection, gain, ids, gates, keys, values, mixed, sems = scratch
    slots = cache.shape[0]
    group, features = queries.shape
    parts = HEAD_PARTS
    wide = features // parts
    small = [(ids_in, ids), (gates_in, gates), (gain_in, gain)]
    first = [(new_kv, newest), (queries, queried)]
    spans = [pl.ds(i * wide, wide) for i in range(parts)]
    pairs = small + first + [(cache.at[:, :, span], cached.at[:, :, span]) for span in spans]
    pairs += [(residual, resid)] + [(out_weight.at[span], projection.at[span]) for span in spans]
    loads = [pltpu.make_async_copy(source, target, sems.at[i]) for i, (source, target) in enumerate(pairs)]
    for load in loads:
        load.start()
    load_small, load_first, load_cache = loads[:3], loads[3:5], loads[5 : 5 + parts]
    load_resid, load_projection = loads[5 + parts], loads[6 + parts :]

    def split(source, start, target, span):
        both = jnp.swapaxes(source[pl.ds(start, 16), :, span], 0, 1)
        keys[pl.ds(target, 16), span] = both[0]
        values[pl.ds(target, 16), span] = both[1]

    for load in load_small:
        load.wait()
    weights = routing(ids[...], gates[...], experts)
    high = weights.astype(jnp.bfloat16)
    low = (weights - high.astype(jnp.float32)).astype(jnp.bfloat16)
    spare = payload.shape[1] - features - 2 * experts
    trail = [high, low] + ([jnp.zeros((group, spare), jnp.bfloat16)] if spare else [])
    payload[:, features:] = jnp.concatenate(trail, axis=1)
    for load in load_first:
        load.wait()
    for i in range(group // 16):
        split(newest, i * 16, slots + i * 16, slice(None))
    positions = slots + group
    slot_place = lax.broadcasted_iota(jnp.int32, (1, positions), 1)
    counted = (slot_place < length[0]) | (slot_place >= slots)
    heads_part = HEADS // parts
    for part in range(parts):
        load_cache[part].wait()
        span = slice(part * wide, (part + 1) * wide)

        def step(k, carry):
            start = pl.multiple_of(k * 16, 16)
            split(cached, start, start, span)
            return carry

        lax.fori_loop(0, slots // 16, step, 0, unroll=4)
        heads = [slice(h * HEAD_DIM, (h + 1) * HEAD_DIM) for h in range(part * heads_part, (part + 1) * heads_part)]
        scores = jnp.concatenate(
            [
                lax.dot_general(
                    queried[:, head], keys[:, head], (((1,), (1,)), ((), ())), preferred_element_type=jnp.float32
                )
                for head in heads
            ],
            axis=0,
        ) * HEAD_DIM ** (-0.5)
        scores = jnp.where(counted, scores, masked_value)
        raised = jnp.exp(scores - jnp.max(scores, axis=-1, keepdims=True))
        softmax_bf = (raised / jnp.sum(raised, axis=-1, keepdims=True)).astype(jnp.bfloat16)
        for i, head in enumerate(heads):
            mixed[:, head] = dot(softmax_bf[i * group : (i + 1) * group], values[:, head]).astype(jnp.bfloat16)
    load_resid.wait()
    total = resid[...].astype(jnp.float32)
    for part in range(parts):
        load_projection[part].wait()
        span = slice(part * wide, (part + 1) * wide)
        total = total + dot(mixed[:, span], projection[span, :])
    stream[...] = total
    mean_square = jnp.mean(total * total, axis=-1, keepdims=True)
    rows = (total * lax.rsqrt(mean_square + 1e-06) * gain[...]).astype(jnp.bfloat16)
    payload[:, :features] = rows
    gather_rows(rows, weights, chips, capacity, outs)


def gather_kernel(chips, capacity, experts, features, payload, *outs):
    weights = unpacked(payload, features, experts)
    gather_rows(payload[:, :features], weights, chips, capacity, outs)


def expert_kernel(capacity, counts, span, length, cached, newest, *refs):
    if span is None or span[0] > 0:
        refs = refs[1:]
    ins, halves, outs = refs[:counts], refs[counts : counts + 6], refs[counts + 6 : -2]
    appended, sem = refs[-2:]
    if span is None:
        write = pltpu.make_async_copy(newest, appended.at[pl.ds(length[0], newest.shape[0])], sem)
    else:
        piece = pl.ds(span[0], span[1] - span[0])
        write = pltpu.make_async_copy(cached.at[piece], appended.at[piece], sem)
    write.start()
    rows = stacked(ins)
    total = None
    for i in range(2):
        gate_half, up_half, down_half = halves[3 * i : 3 * i + 3]
        gate_act = dot(rows, gate_half[...])
        hidden = (gate_act / (1.0 + jnp.exp(-gate_act)) * dot(rows, up_half[...])).astype(jnp.bfloat16)
        partial = dot(hidden, down_half[...])
        total = partial if total is None else total + partial
    scatter_out(total, capacity, outs)
    write.wait()


def combine_kernel(counts, table, *refs):
    total = combined(refs[:counts], table)
    for ref in refs[counts:-1]:
        total = total + ref[...].astype(jnp.float32)
    refs[-1][...] = total.astype(jnp.bfloat16)


def own_kernel(table, stream, *refs):
    refs[-1][...] = stream[...] + combined(refs[:-1], table)


def in_vmem(count):
    return [pl.BlockSpec(memory_space=VMEM)] * count


SMEM_SPEC = pl.BlockSpec(memory_space=pltpu.SMEM)
HBM_SPEC = pl.BlockSpec(memory_space=pltpu.HBM)


ORDER = (("in", 0), ("out", 0), ("in", 3), ("in", 1), ("out", 3), ("in", 2), ("out", 2), ("out", 1))
LAG = 2
DUE = {}


def shards(
    queries, new_kv, cache, lengths, residual, out_weight, norm_gain, expert_ids, gates, w_gate, w_up, w_down,
):
    planes, chips, cores = (lax.axis_size(axis) for axis in ALL)
    experts = planes * chips
    group, features = queries.shape[1:]
    slots = cache.shape[1]
    top_k = expert_ids.shape[2]
    capacity = 5 * group * top_k // (4 * experts)
    tiled = capacity % 8 == 0
    bf16 = jnp.bfloat16
    width = features + -(-2 * experts // 128) * 128

    def params(mib):
        return pltpu.CompilerParams(vmem_limit_bytes=mib << 20)

    def across(x, axis, j):
        size = lax.axis_size(axis)
        return lax.ppermute(x, axis, [(i, i ^ j) for i in range(size)])

    def to_chips(blocks):
        return [blocks[0]] + [across(blocks[j], "chip", j) for j in range(1, chips)]

    if tiled:
        block_shapes = [jax.ShapeDtypeStruct((capacity, features), bf16)] * chips
    else:
        block_shapes = [jax.ShapeDtypeStruct((chips * capacity, features), bf16)]
    blocks_n = len(block_shapes)
    table_shape = jax.ShapeDtypeStruct((2 * group, chips * capacity), bf16)

    def cut(blocks):
        return blocks if tiled else [blocks[0][j * capacity : (j + 1) * capacity] for j in range(chips)]

    def joined(blocks):
        return blocks if tiled else [jnp.concatenate(blocks, axis=0)]

    own_halves = [w_gate[0], w_up[0], w_down[0]]
    other_halves = [across(half, "core", 1) for half in own_halves]

    stream, payload, cached, newest, table, *outgoing = pl.pallas_call(
        functools.partial(attention_kernel, chips, capacity, experts),
        out_shape=[
            jax.ShapeDtypeStruct((group, features), jnp.float32),
            jax.ShapeDtypeStruct((group, width), bf16),
            jax.ShapeDtypeStruct(cache.shape[1:], bf16),
            jax.ShapeDtypeStruct(new_kv.shape[1:], bf16),
            table_shape,
        ]
        + block_shapes,
        in_specs=[SMEM_SPEC] + [HBM_SPEC] * 8,
        out_specs=in_vmem(5 + blocks_n),
        scratch_shapes=[
            VMEM((group, features), bf16),
            VMEM((group, features), bf16),
            VMEM(out_weight.shape, bf16),
            VMEM((1, features), jnp.float32),
            VMEM((top_k, group), jnp.int32),
            VMEM((top_k, group), jnp.float32),
            VMEM((slots + group, features), bf16),
            VMEM((slots + group, features), bf16),
            VMEM((group, features), bf16),
            pltpu.SemaphoreType.DMA((6 + 2 * HEAD_PARTS,)),
        ],
        compiler_params=params(24),
        cost_estimate=pl.CostEstimate(
            flops=12_000_000_000, bytes_accessed=24 * features * features // 4, transcendentals=0
        ),
        name="attention",
    )(
        lengths,
        *[
            pltpu.with_memory_space_constraint(x, pltpu.HBM)
            for x in (
                queries[0], new_kv[0], cache[0], residual[0], out_weight, norm_gain[None], expert_ids[0].T, gates[0].T,
            )
        ],
    )

    payload, outgoing, other_halves = lax.optimization_barrier((payload, outgoing, other_halves))
    halves = [pltpu.with_memory_space_constraint(half, VMEM) for half in own_halves + other_halves]

    def gather(packed):
        return pl.pallas_call(
            functools.partial(gather_kernel, chips, capacity, experts, features),
            out_shape=[table_shape] + block_shapes,
            in_specs=in_vmem(1),
            out_specs=in_vmem(1 + blocks_n),
            compiler_params=params(8),
            name="gather",
        )(packed)

    held = [pltpu.with_memory_space_constraint(x, VMEM) for x in (cached, newest)]
    cuts = [slots * i // (planes - 1) for i in range(planes)]
    spans = list(zip(cuts[:-1], cuts[1:])) + [None]

    def run_experts(arrived, call, appended):
        before = [] if call == 0 else [pltpu.with_memory_space_constraint(appended, pltpu.HBM)]
        *results, appended = pl.pallas_call(
            functools.partial(expert_kernel, capacity, blocks_n, spans[call]),
            out_shape=block_shapes + [jax.ShapeDtypeStruct(cache.shape[1:], cache.dtype)],
            in_specs=[SMEM_SPEC] + in_vmem(2) + [HBM_SPEC] * len(before) + in_vmem(blocks_n + 6),
            out_specs=in_vmem(blocks_n) + [HBM_SPEC],
            scratch_shapes=[pltpu.SemaphoreType.DMA],
            input_output_aliases={3: blocks_n} if before else {},
            compiler_params=params(8),
            cost_estimate=pl.CostEstimate(
                flops=12 * chips * capacity * features * w_gate.shape[2],
                bytes_accessed=12 * features * w_gate.shape[2],
                transcendentals=0,
            ),
            name="experts",
        )(lengths, *held, *before, *arrived, *halves)
        return results, appended

    def combine(packed, returned, extra):
        return pl.pallas_call(
            functools.partial(combine_kernel, blocks_n),
            out_shape=jax.ShapeDtypeStruct((group, features), bf16),
            in_specs=in_vmem(1 + blocks_n + len(extra)),
            out_specs=pl.BlockSpec(memory_space=VMEM),
            compiler_params=params(8),
            name="combine",
        )(packed, *returned, *extra)

    payload_of = {0: payload, 1: across(payload, "req", 1), 3: across(payload, "req", 3)}
    payload_of[2] = across(payload_of[3], "req", 1)
    calls, appended, table_of = 0, None, {}
    arrived_of, returned_of, partials, moved = {}, {}, {}, []

    def send_back(s, hold):
        extra = [partials.pop(3)] if s == 2 else []
        partial = combine(table_of[s], returned_of.pop(s), extra)
        hold, partial = lax.optimization_barrier((hold, partial))
        partials[s] = across(partial, "req", 2 if s == 2 else 1)
        return hold

    for k, (way, s) in enumerate(ORDER):
        if way == "in":
            if s == 0:
                blocks = outgoing
            else:
                table_of[s], *blocks = gather(payload_of[s])
        else:
            blocks, appended = run_experts(arrived_of[s], calls, appended)
            calls += 1
        if k >= LAG:
            pw, ps = ORDER[k - LAG]
            if pw == "out" and ps > 0:
                blocks = send_back(ps, blocks)
            else:
                blocks, got = lax.optimization_barrier((blocks, moved[k - LAG]))
                (arrived_of if pw == "in" else returned_of)[ps] = got
        if k in DUE:
            blocks, partials[DUE[k]] = lax.optimization_barrier((blocks, partials[DUE[k]]))
        got = joined(to_chips(cut(blocks)))
        moved.append(got)
        (arrived_of if way == "in" else returned_of)[s] = got
    for way, s in ORDER:
        if way == "out" and s > 0 and s in returned_of:
            send_back(s, ())
    own_returned = returned_of[0]
    total = pl.pallas_call(
        own_kernel,
        out_shape=jax.ShapeDtypeStruct((group, features), jnp.float32),
        in_specs=in_vmem(2 + blocks_n),
        out_specs=pl.BlockSpec(memory_space=VMEM),
        compiler_params=params(8),
        name="own",
    )(table, stream, *own_returned)
    for partial in partials.values():
        total = total + partial.astype(jnp.float32)
    layer_out = total.astype(bf16)
    return (layer_out[None], appended[None])


def solution(mesh):
    planes, width = (mesh.shape[axis] for axis in ("req", "exp"))
    split = Mesh(mesh.devices.reshape(planes, width // 2, 2), ALL)
    by_device = P(ALL)
    placed = (by_device,) * 5 + (P(), P()) + (by_device,) * 5
    return jax.shard_map(
        shards,
        mesh=split,
        in_specs=placed,
        out_specs=(by_device, by_device),
        check_vma=False,
    )
```
